128 devices in a mesh: dp: 32 (over y, x, core), mp: 4 (over z).
Axes of the slice: x: 4, y: 4, z: 4, core: 2. Of those that a mesh axis runs over, the one named last changes fastest.
Arguments:
- tokens: bfloat16 [65536, 768], P('dp'), may hold values from -6 to 6
- time_emb: bfloat16 [512, 768], P('dp'), may hold values from -3 to 3
- segments: int32 [512, 128], P('dp'), may hold values from 0 to 3, never falling along the last dimension, each value on 1 to 64 neighbouring positions
- cotangent: bfloat16 [65536, 768], P('dp')
- w_qkv: float32 [3, 768, 768], P(None, 'dp', 'mp'), may hold values from -0.21875 to 0.21875
- w_out: float32 [768, 768], P('mp', 'dp')
- w_up: float32 [768, 3072], P('dp', 'mp'), may hold values from -0.21875 to 0.21875
- w_down: float32 [3072, 768], P('mp', 'dp')
- norm_params: float32 [4, 768], P(None, 'dp')
- qkv_first: float32 [3, 768, 768], P(None, 'dp', 'mp')
- qkv_second: float32 [3, 768, 768], P(None, 'dp', 'mp')
- out_first: float32 [768, 768], P('mp', 'dp')
- out_second: float32 [768, 768], P('mp', 'dp')
- up_first: float32 [768, 3072], P('dp', 'mp')
- up_second: float32 [768, 3072], P('dp', 'mp')
- down_first: float32 [3072, 768], P('mp', 'dp')
- down_second: float32 [3072, 768], P('mp', 'dp')
- norm_first: float32 [4, 768], P(None, 'dp')
- norm_second: float32 [4, 768], P(None, 'dp')
Outputs:
- layer_out: bfloat16 [65536, 768], P('dp')
- input_grad: bfloat16 [65536, 768], P('dp')
- grad_norm: float32 [], replicated
- qkv_moment: float32 [3, 768, 768], P(None, 'dp', 'mp')
- qkv_square: float32 [3, 768, 768], P(None, 'dp', 'mp')
- qkv_weight: float32 [3, 768, 768], P(None, 'dp', 'mp')
- out_moment: float32 [768, 768], P('mp', 'dp')
- out_square: float32 [768, 768], P('mp', 'dp')
- out_weight: float32 [768, 768], P('mp', 'dp')
- up_moment: float32 [768, 3072], P('dp', 'mp')
- up_square: float32 [768, 3072], P('dp', 'mp')
- up_weight: float32 [768, 3072], P('dp', 'mp')
- down_moment: float32 [3072, 768], P('mp', 'dp')
- down_square: float32 [3072, 768], P('mp', 'dp')
- down_weight: float32 [3072, 768], P('mp', 'dp')
- norm_moment: float32 [4, 768], P(None, 'dp')
- norm_square: float32 [4, 768], P(None, 'dp')
- norm_value: float32 [4, 768], P(None, 'dp')
- norm_grad: float32 [4, 768], P(None, 'dp')
The draws below stay inside these ranges and needn't reach their ends.
Inputs may be any that keep to these rules, and one draw needn't show every extreme that they name: `segments`: along each packed row of 128 positions the segment numbers never fall, and a segment holds at most 64 positions.
All inputs are finite; a program needn't handle non-finite values.
Results may differ from the reference program's by a relative error of at most 0.02.
Values may be sent and summed in bfloat16 or wider, within the bound.
A program may use at most 128 MiB of HBM per device.

```python
import math
import jax
import jax.numpy as jnp
import numpy as np
from jax import lax

D = 768
HEADS = 12
HEAD = 64
FF = 3072
LEN = 128
STEP = 10
SEQUENCES = 512
TOKENS = 65536


CLIP_AT = 1.0


BETA_ONE = 0.9


BETA_TWO = 0.95


def ramp_line(count, low_end, high_end):
    position = jnp.arange(count, dtype=jnp.float32) / max(count - 1, 1)
    return low_end * (high_end / low_end) ** position


def ramp_ends():
    return (0.6, 1.8)


def typical_grad():
    param_count = 4 * D * HEADS * HEAD + 2 * D * FF + 4 * D
    return CLIP_AT / math.sqrt(param_count)


def first_draw(key, shape, typical):
    return (1.0 - BETA_ONE) / BETA_ONE * typical * jax.random.normal(key, shape, jnp.float32)


def second_draw(key, shape, typical):
    spread = jnp.exp(jax.random.uniform(key, shape, jnp.float32, minval=0.0, maxval=math.log(4.0)))
    return (1.0 - BETA_TWO) / BETA_TWO * typical * typical * spread


def draw_cotangent(key, part):
    key = jax.random.fold_in(key, 3)
    low_end, high_end = ramp_ends()
    noise = jax.random.normal(key, (TOKENS, D), jnp.float32)
    return (noise * ramp_line(D, low_end, high_end)[None, :]).astype(jnp.bfloat16)


def draw_w_out(key, part):
    key = jax.random.fold_in(key, 5)
    low_end, high_end = ramp_ends()
    noise = jax.random.truncated_normal(key, -3.0, 3.0, (HEADS * HEAD, D), jnp.float32)
    sizing = math.sqrt(max(LEN // 4, 1)) / math.sqrt(HEADS * HEAD)
    return noise * ramp_line(HEADS * HEAD, low_end, high_end)[:, None] * sizing


def draw_w_down(key, part):
    key = jax.random.fold_in(key, 7)
    low_end, high_end = ramp_ends()
    noise = jax.random.truncated_normal(key, -3.0, 3.0, (FF, D), jnp.float32)
    return noise * ramp_line(FF, low_end, high_end)[:, None] / math.sqrt(FF)


def draw_norm_params(key, part):
    key = jax.random.fold_in(key, 11)
    low_end, high_end = ramp_ends()
    gain_key, shift_key = jax.random.split(key)
    gain_noise = jax.random.uniform(gain_key, (4, D), jnp.float32, minval=-1.7, maxval=1.7)
    shift_noise = jax.random.uniform(shift_key, (4, D), jnp.float32, minval=-0.8, maxval=0.8)
    gains = ramp_line(D, low_end, high_end)[None, :] * (1.0 + 0.1 * gain_noise)
    return jnp.stack([gains[0], shift_noise[1], gains[2], shift_noise[3]])


def draw_qkv_first(key, part):
    key = jax.random.fold_in(key, 21)
    return first_draw(key, (3, D, HEADS * HEAD), typical_grad())


def draw_qkv_second(key, part):
    key = jax.random.fold_in(key, 22)
    return second_draw(key, (3, D, HEADS * HEAD), typical_grad())


def draw_out_first(key, part):
    key = jax.random.fold_in(key, 23)
    return first_draw(key, (HEADS * HEAD, D), typical_grad())


def draw_out_second(key, part):
    key = jax.random.fold_in(key, 24)
    return second_draw(key, (HEADS * HEAD, D), typical_grad())


def draw_up_first(key, part):
    key = jax.random.fold_in(key, 25)
    return first_draw(key, (D, FF), typical_grad())


def draw_up_second(key, part):
    key = jax.random.fold_in(key, 26)
    return second_draw(key, (D, FF), typical_grad())


def draw_down_first(key, part):
    key = jax.random.fold_in(key, 27)
    return first_draw(key, (FF, D), typical_grad())


def draw_down_second(key, part):
    key = jax.random.fold_in(key, 28)
    return second_draw(key, (FF, D), typical_grad())


def draw_norm_first(key, part):
    key = jax.random.fold_in(key, 29)
    return first_draw(key, (4, D), 3.0 * typical_grad())


def draw_norm_second(key, part):
    key = jax.random.fold_in(key, 30)
    return second_draw(key, (4, D), 3.0 * typical_grad())


def block_scale(key, dims, cuts, least, top_value):
    level = 1.0
    for axis_at, shards_of in cuts:
        heights = jax.random.uniform(jax.random.fold_in(jax.random.fold_in(key, 6), axis_at), (shards_of,), jnp.float32, least / len(cuts), top_value / len(cuts))
        level = level * jnp.repeat(jnp.exp(heights), dims[axis_at] // shards_of).reshape((-1,) + (1,) * (len(dims) - 1 - axis_at))
    return level


def split_up(amount, total, bound, slope):
    weights = [(1 << 20) // math.isqrt(rank ** slope) + 1 for rank in range(2, amount + 1)]
    spare, given = total - bound - (amount - 1), [1] * (amount - 1)
    while spare > 0:
        candidates = [i for i in range(amount - 1) if given[i] < bound]
        whole, budget = sum([weights[i] for i in candidates]), spare
        for i in candidates:
            extra = min(bound - given[i], max(1, budget * weights[i] // whole), spare)
            given[i] = given[i] + extra
            spare = spare - extra
    return np.array([bound] + given)


def ragged(stream_key, count, total, reach, slope):
    if count == 2:
        one = jax.random.randint(stream_key, (), max(1, total - reach), min(reach, total - 1) + 1)
        return jnp.stack([one, total - one])
    tallies = jnp.asarray(split_up(count, total, reach, slope), jnp.int32)
    twos = (count - 1) // 2
    donor, receiver = tallies[1:1 + 2 * twos:2], tallies[2:2 + 2 * twos:2]
    room = jnp.minimum(donor - 1, reach - receiver)
    moved = jax.random.randint(jax.random.fold_in(stream_key, 1), (twos,), 0, 1 << 20) % (room + 1)
    tallies = tallies.at[1:1 + 2 * twos:2].set(donor - moved).at[2:2 + 2 * twos:2].set(receiver + moved)
    return tallies[jax.random.permutation(jax.random.fold_in(stream_key, 2), count)]


def bell_draw(own_key, extent, scale, reach, shards=(), held_as=jnp.bfloat16):
    factor_of = block_scale(own_key, extent, shards, -0.22, 0.18) if shards else 1.0
    values = jax.random.normal(own_key, extent, jnp.float32) * scale * factor_of
    return jnp.minimum(jnp.maximum(values, -reach), reach).astype(held_as)


def setup_inputs(seed: int = 0) -> dict:
    splits = jax.random.split(jax.random.key(seed), 20)
    return {
        "tokens": bell_draw(splits[0], (TOKENS, D), 1.0, 6.0, ((0, 32),)),
        "time_emb": bell_draw(splits[1], (SEQUENCES, D), 0.5, 3.0, ((0, 32),)),
        "segments": jax.vmap(lambda own: jnp.searchsorted(jnp.cumsum(ragged(own, 4, LEN, LEN // 2, 0)), jnp.arange(LEN), side="right"))(jax.random.split(splits[2], SEQUENCES)).reshape((SEQUENCES, LEN)).astype(jnp.int32),
        "cotangent": draw_cotangent(jax.random.fold_in(splits[19], 71), 0),
        "w_qkv": bell_draw(splits[4], (3, D, HEADS * HEAD), D ** -0.5, 0.21875, ((1, 32), (2, 4)), jnp.float32),
        "w_out": draw_w_out(jax.random.fold_in(splits[19], 71), 0),
        "w_up": bell_draw(splits[6], (D, FF), D ** -0.5, 0.21875, ((0, 32), (1, 4)), jnp.float32),
        "w_down": draw_w_down(jax.random.fold_in(splits[19], 71), 0),
        "norm_params": draw_norm_params(jax.random.fold_in(splits[19], 71), 0),
        "qkv_first": draw_qkv_first(jax.random.fold_in(splits[19], 71), 0),
        "qkv_second": draw_qkv_second(jax.random.fold_in(splits[19], 71), 0),
        "out_first": draw_out_first(jax.random.fold_in(splits[19], 71), 0),
        "out_second": draw_out_second(jax.random.fold_in(splits[19], 71), 0),
        "up_first": draw_up_first(jax.random.fold_in(splits[19], 71), 0),
        "up_second": draw_up_second(jax.random.fold_in(splits[19], 71), 0),
        "down_first": draw_down_first(jax.random.fold_in(splits[19], 71), 0),
        "down_second": draw_down_second(jax.random.fold_in(splits[19], 71), 0),
        "norm_first": draw_norm_first(jax.random.fold_in(splits[19], 71), 0),
        "norm_second": draw_norm_second(jax.random.fold_in(splits[19], 71), 0),
    }


@jax.custom_vjp
def low(v):
    return lax.optimization_barrier(v.astype(jnp.bfloat16)).astype(jnp.float32)

@jax.custom_vjp
def low_back(v):
    return v

def low_keep(v):
    return (low(v), None)

def low_pass(kept, grad):
    return (grad,)

def back_keep(v):
    return (v, None)

def back_low(kept, grad):
    return (low(grad),)
low.defvjp(low_keep, low_pass)
low_back.defvjp(back_keep, back_low)
NORM_EPS = 1e-05
CLIP_AT = 1.0
BETA_ONE = 0.9
BETA_TWO = 0.95
ADAM_EPS = 1e-08
WEIGHT_DECAY = 0.01
RATE_MATRIX = 0.05
RATE_OUT = 0.3
RATE_VECTOR = 0.5
PRECISE = lax.Precision.HIGHEST

def layer_norm(values, gain, shift):
    center = lax.optimization_barrier(jnp.mean(values, axis=-1, keepdims=True))
    offset = values - center
    spread = lax.optimization_barrier(jnp.mean(offset * offset, axis=-1, keepdims=True))
    return offset * lax.rsqrt(spread + NORM_EPS) * gain + shift

def attend(queries, key_rows, value_rows, labels):
    scaling = HEAD ** (-0.5)
    scores = jnp.einsum('bqhe,bkhe->bhqk', queries, key_rows, precision=PRECISE) * scaling
    scores = low_back(scores)
    allowed = labels[:, None, :, None] == labels[:, None, None, :]
    scores = jnp.where(allowed, scores, -1e+30)
    highest = lax.optimization_barrier(jnp.max(scores, axis=-1, keepdims=True))
    exponent = jnp.exp(scores - highest)
    probs_full = low(exponent / lax.optimization_barrier(jnp.sum(exponent, axis=-1, keepdims=True)))
    return jnp.einsum('bhqk,bkhe->bqhe', probs_full, value_rows, precision=PRECISE)

def attend_block(pieces):
    return attend(pieces[0], pieces[1], pieces[2], pieces[3])

def forward(hidden_in, time_rows, w_qkv, w_out, w_up, w_down, norm_params, segments):
    seq_count = segments.shape[0]
    all_width = HEADS * HEAD
    start_rows = hidden_in + jnp.repeat(time_rows, LEN, axis=0)
    gain_rows = low(norm_params)
    normed = low(layer_norm(start_rows, gain_rows[0], gain_rows[1]))
    project = jnp.einsum('td,cdf->ctf', normed, low(w_qkv), precision=PRECISE)
    project = low_back(low(project))
    group_size = math.gcd(seq_count, max(1, 4096 // LEN))
    blocks = seq_count // group_size
    shaped = project.reshape(3, blocks, group_size, LEN, HEADS, HEAD)
    labels = segments.reshape(blocks, group_size, LEN)
    mixed_heads = lax.map(jax.checkpoint(attend_block), (shaped[0], shaped[1], shaped[2], labels))
    mixed_heads = low_back(low(mixed_heads.reshape(seq_count * LEN, all_width)))
    middle = start_rows + low_back(jnp.dot(mixed_heads, low(w_out), precision=PRECISE))
    normed_two = low(layer_norm(middle, gain_rows[2], gain_rows[3]))
    before = low_back(jnp.dot(normed_two, low(w_up), precision=PRECISE))
    active = low(jax.nn.gelu(before, approximate=False))
    return middle + jnp.dot(active, low(w_down), precision=PRECISE)

def adam_step(weight, gradient, moment, second, step_rate, decay_rate):
    moment = BETA_ONE * moment + (1.0 - BETA_ONE) * gradient
    second = BETA_TWO * second + (1.0 - BETA_TWO) * gradient * gradient
    moment_hat = moment / (1.0 - BETA_ONE ** STEP)
    second_hat = second / (1.0 - BETA_TWO ** STEP)
    weight = weight - step_rate * (moment_hat / (jnp.sqrt(second_hat) + ADAM_EPS) + decay_rate * weight)
    return (moment, second, weight)

def reference(tokens, time_emb, segments, cotangent, w_qkv, w_out, w_up, w_down, norm_params, qkv_first, qkv_second, out_first, out_second, up_first, up_second, down_first, down_second, norm_first, norm_second):
    hidden_in = tokens.astype(jnp.float32)
    time_rows = time_emb.astype(jnp.float32)

    def layer_fn(hidden_arg, qkv_arg, out_arg, up_arg, down_arg, norm_arg):
        return forward(hidden_arg, time_rows, qkv_arg, out_arg, up_arg, down_arg, norm_arg, segments)
    result, pullback = jax.vjp(layer_fn, hidden_in, w_qkv, w_out, w_up, w_down, norm_params)
    gradients = pullback(cotangent.astype(jnp.float32))
    squares = jnp.zeros((), jnp.float32)
    for grad_part in gradients[1:]:
        squares = squares + jnp.sum(grad_part * grad_part)
    grad_norm = jnp.sqrt(squares)
    factor = jnp.minimum(1.0, CLIP_AT / (grad_norm + 1e-06))
    norm_grad = gradients[5] * factor
    qkv_new = adam_step(w_qkv, gradients[1] * factor, qkv_first, qkv_second, RATE_MATRIX, WEIGHT_DECAY)
    out_new = adam_step(w_out, gradients[2] * factor, out_first, out_second, RATE_OUT, WEIGHT_DECAY)
    up_new = adam_step(w_up, gradients[3] * factor, up_first, up_second, RATE_MATRIX, WEIGHT_DECAY)
    down_new = adam_step(w_down, gradients[4] * factor, down_first, down_second, RATE_MATRIX, WEIGHT_DECAY)
    norm_new = adam_step(norm_params, norm_grad, norm_first, norm_second, RATE_VECTOR, 0.0)
    return (result.astype(jnp.bfloat16), gradients[0].astype(jnp.bfloat16), grad_norm, qkv_new[0], qkv_new[1], qkv_new[2], out_new[0], out_new[1], out_new[2], up_new[0], up_new[1], up_new[2], down_new[0], down_new[1], down_new[2], norm_new[0], norm_new[1], norm_new[2], norm_grad)
```

```python
import jax
import jax.numpy as jnp
from jax import lax
from jax.sharding import PartitionSpec as P

HEAD = 64
QKV = 192
HIDDEN = 768
STEP = 10


NORM_EPS = 1e-05
CLIP_AT = 1.0
BETA_ONE = 0.9
BETA_TWO = 0.95
ADAM_EPS = 1e-08
WEIGHT_DECAY = 0.01
RATE_MATRIX = 0.05
RATE_OUT = 0.3
RATE_VECTOR = 0.5


def norm_parts(values, gain, shift):
    center = jnp.mean(values, axis=-1, keepdims=True)
    offset = values - center
    spread = jnp.mean(offset * offset, axis=-1, keepdims=True)
    inverse = lax.rsqrt(spread + NORM_EPS)
    scaled = offset * inverse
    return (scaled * gain + shift, scaled, inverse)


def norm_back(grad_rows, scaled, inverse, gain):
    through = grad_rows * gain
    first_mean = jnp.mean(through, axis=-1, keepdims=True)
    second_mean = jnp.mean(through * scaled, axis=-1, keepdims=True)
    grad_in = inverse * (through - first_mean - scaled * second_mean)
    return (grad_in, jnp.sum(grad_rows * scaled, axis=0), jnp.sum(grad_rows, axis=0))


def left_product(first_arr, second_arr):
    return lax.dot_general(
        first_arr, second_arr, (((0,), (0,)), ((), ())), preferred_element_type=jnp.float32
    )


def right_product(first_arr, second_arr):
    return lax.dot_general(
        first_arr, second_arr, (((1,), (1,)), ((), ())), preferred_element_type=jnp.float32
    )


def exact_gelu(values):
    return jax.nn.gelu(values, approximate=False)


def masked_scores(queries, key_rows, allowed):
    scaling = HEAD ** (-0.5)
    scores = (
        jnp.einsum("bqhe,bkhe->bhqk", queries, key_rows, preferred_element_type=jnp.float32)
        * scaling
    )
    return jnp.where(allowed, scores, -1e30)


def layer_pass(weights, gain_rows, tokens_part, time_part, labels, grad_rows):
    seq_count, length = labels.shape
    row_count = seq_count * length
    blocks = weights.shape[0]
    model = weights.shape[1]
    w_qkv = weights[:, :, : 3 * QKV].reshape(blocks, model, 3, QKV)
    w_out = weights[:, :, 3 * QKV : 4 * QKV]
    w_up = weights[:, :, 4 * QKV : 4 * QKV + HIDDEN]
    w_down = weights[:, :, 4 * QKV + HIDDEN :]
    scaling = HEAD ** (-0.5)
    heads = QKV // HEAD
    start_rows = tokens_part.astype(jnp.float32) + jnp.repeat(
        time_part.astype(jnp.float32), length, axis=0
    )
    normed, scaled_one, inverse_one = norm_parts(start_rows, gain_rows[0], gain_rows[1])
    normed = normed.astype(jnp.bfloat16)
    project = jnp.einsum(
        "td,mdcf->cmtf", normed, w_qkv, preferred_element_type=jnp.float32
    ).astype(jnp.bfloat16)
    shaped = project.reshape(3, blocks, seq_count, length, heads, HEAD)
    queries, key_rows, value_rows = (shaped[0], shaped[1], shaped[2])
    allowed = labels[:, :, None] == labels[:, None, :]
    allowed = allowed[None, :, None, :, :]
    scores = (
        jnp.einsum("mbqhe,mbkhe->mbhqk", queries, key_rows, preferred_element_type=jnp.float32)
        * scaling
    )
    scores = jnp.where(allowed, scores, -1e30)
    highest = jnp.max(scores, axis=-1, keepdims=True)
    exponent = jnp.exp(scores - highest)
    totals = jnp.sum(exponent, axis=-1, keepdims=True)
    probs_full = exponent / totals
    probs_low = probs_full.astype(jnp.bfloat16)
    mixed_heads = jnp.einsum(
        "mbhqk,mbkhe->mbqhe", probs_low, value_rows, preferred_element_type=jnp.float32
    )
    mixed_heads = mixed_heads.astype(jnp.bfloat16).reshape(blocks, row_count, QKV)
    middle = start_rows + jnp.einsum(
        "mtf,mdf->td", mixed_heads, w_out, preferred_element_type=jnp.float32
    )
    normed_two, scaled_two, inverse_two = norm_parts(middle, gain_rows[2], gain_rows[3])
    normed_two = normed_two.astype(jnp.bfloat16)
    before = jnp.einsum("td,mdf->mtf", normed_two, w_up, preferred_element_type=jnp.float32)
    active, gelu_pull = jax.vjp(exact_gelu, before)
    active = active.astype(jnp.bfloat16)
    result = middle + jnp.einsum(
        "mtf,mdf->td", active, w_down, preferred_element_type=jnp.float32
    )
    grad_down = jnp.einsum("td,mtf->mdf", grad_rows, active, preferred_element_type=jnp.float32)
    grad_active = jnp.einsum("td,mdf->mtf", grad_rows, w_down, preferred_element_type=jnp.float32)
    (grad_before,) = gelu_pull(grad_active)
    grad_before = grad_before.astype(jnp.bfloat16)
    grad_up = jnp.einsum("td,mtf->mdf", normed_two, grad_before, preferred_element_type=jnp.float32)
    grad_normed_two = jnp.einsum(
        "mtf,mdf->td", grad_before, w_up, preferred_element_type=jnp.float32
    )
    back_two, gain_two, shift_two = norm_back(
        grad_normed_two, scaled_two, inverse_two, gain_rows[2]
    )
    grad_middle = grad_rows.astype(jnp.float32) + back_two
    branch_low = grad_middle.astype(jnp.bfloat16)
    grad_out = jnp.einsum(
        "td,mtf->mdf", branch_low, mixed_heads, preferred_element_type=jnp.float32
    )
    grad_mixed = jnp.einsum(
        "td,mdf->mtf", branch_low, w_out, preferred_element_type=jnp.float32
    ).astype(jnp.bfloat16)
    grad_mixed = grad_mixed.reshape(blocks, seq_count, length, heads, HEAD)
    grad_value = jnp.einsum(
        "mbhqk,mbqhe->mbkhe", probs_low, grad_mixed, preferred_element_type=jnp.float32
    ).astype(jnp.bfloat16)
    grad_probs = jnp.einsum(
        "mbqhe,mbkhe->mbhqk", grad_mixed, value_rows, preferred_element_type=jnp.float32
    )
    row_inner = jnp.sum(grad_probs * probs_full, axis=-1, keepdims=True)
    grad_scores = (probs_full * (grad_probs - row_inner)).astype(jnp.bfloat16)
    grad_query = (
        jnp.einsum("mbhqk,mbkhe->mbqhe", grad_scores, key_rows, preferred_element_type=jnp.float32)
        * scaling
    ).astype(jnp.bfloat16)
    grad_key = (
        jnp.einsum("mbhqk,mbqhe->mbkhe", grad_scores, queries, preferred_element_type=jnp.float32)
        * scaling
    ).astype(jnp.bfloat16)
    grad_project = jnp.stack([grad_query, grad_key, grad_value]).reshape(
        3, blocks, row_count, QKV
    )
    grad_qkv = jnp.einsum(
        "td,cmtf->mdcf", normed, grad_project, preferred_element_type=jnp.float32
    ).reshape(blocks, model, 3 * QKV)
    grad_normed = jnp.einsum(
        "cmtf,mdcf->td", grad_project, w_qkv, preferred_element_type=jnp.float32
    )
    back_one, gain_one, shift_one = norm_back(grad_normed, scaled_one, inverse_one, gain_rows[0])
    grad_start = grad_middle + back_one
    grad_norm_rows = jnp.stack([gain_one, shift_one, gain_two, shift_two])
    grads = jnp.concatenate([grad_qkv, grad_out, grad_up, grad_down], axis=2)
    return (
        result.astype(jnp.bfloat16),
        grad_start.astype(jnp.bfloat16),
        grads.astype(jnp.bfloat16),
        grad_norm_rows,
    )


def adam_step(weight, gradient, moment, second, step_rate, decay_rate):
    moment = BETA_ONE * moment + (1.0 - BETA_ONE) * gradient
    second = BETA_TWO * second + (1.0 - BETA_TWO) * gradient * gradient
    moment_hat = moment / (1.0 - BETA_ONE**STEP)
    second_hat = second / (1.0 - BETA_TWO**STEP)
    weight = weight - step_rate * (
        moment_hat / (jnp.sqrt(second_hat) + ADAM_EPS) + decay_rate * weight
    )
    return (moment, second, weight)


def body(
    tokens,
    time_emb,
    segments,
    cotangent,
    w_qkv,
    w_out,
    w_up,
    w_down,
    norm_params,
    qkv_first,
    qkv_second,
    out_first,
    out_second,
    up_first,
    up_second,
    down_first,
    down_second,
    norm_first,
    norm_second,
):
    low = jnp.bfloat16
    packed = jnp.concatenate(
        [w_qkv[0], w_qkv[1], w_qkv[2], w_out.T, w_up, w_down.T], axis=1
    ).astype(low)
    weights = lax.all_gather(packed, "mp", axis=0)
    weights = lax.all_gather(weights, "dp", axis=1, tiled=True)
    gain_rows = lax.all_gather(norm_params.astype(low), "dp", axis=1, tiled=True)
    gain_rows = gain_rows.astype(jnp.float32)
    place = lax.axis_index("mp")
    seqs = segments.shape[0] // lax.axis_size("mp")
    rows = tokens.shape[0] // lax.axis_size("mp")
    result, grad_start, grads, grad_norm_rows = layer_pass(
        weights,
        gain_rows,
        lax.dynamic_slice_in_dim(tokens, place * rows, rows),
        lax.dynamic_slice_in_dim(time_emb, place * seqs, seqs),
        lax.dynamic_slice_in_dim(segments, place * seqs, seqs),
        lax.dynamic_slice_in_dim(cotangent, place * rows, rows),
    )
    result = lax.all_gather(result, "mp", axis=0, tiled=True)
    grad_start = lax.all_gather(grad_start, "mp", axis=0, tiled=True)
    grads = lax.psum_scatter(grads, "dp", scatter_dimension=1, tiled=True)
    grads = lax.psum_scatter(grads, "mp", scatter_dimension=0).astype(jnp.float32)
    norm_share = lax.psum(
        lax.psum_scatter(grad_norm_rows, "dp", scatter_dimension=1, tiled=True), "mp"
    )
    edge = 4 * QKV
    shares = (
        jnp.stack([grads[:, :QKV], grads[:, QKV : 2 * QKV], grads[:, 2 * QKV : 3 * QKV]]),
        grads[:, 3 * QKV : edge].T,
        grads[:, edge : edge + HIDDEN],
        grads[:, edge + HIDDEN :].T,
        norm_share,
    )
    mp_count = lax.axis_size("mp")
    squares = jnp.sum(shares[4] * shares[4]) / mp_count
    for grad_part in shares[:4]:
        squares = squares + jnp.sum(grad_part * grad_part)
    grad_norm = jnp.sqrt(lax.psum(squares, ("dp", "mp")))
    factor = jnp.minimum(1.0, CLIP_AT / (grad_norm + 1e-06))
    norm_grad = shares[4] * factor
    qkv_new = adam_step(w_qkv, shares[0] * factor, qkv_first, qkv_second, RATE_MATRIX, WEIGHT_DECAY)
    out_new = adam_step(w_out, shares[1] * factor, out_first, out_second, RATE_OUT, WEIGHT_DECAY)
    up_new = adam_step(w_up, shares[2] * factor, up_first, up_second, RATE_MATRIX, WEIGHT_DECAY)
    down_new = adam_step(
        w_down, shares[3] * factor, down_first, down_second, RATE_MATRIX, WEIGHT_DECAY
    )
    norm_new = adam_step(norm_params, norm_grad, norm_first, norm_second, RATE_VECTOR, 0.0)
    return (
        result,
        grad_start,
        grad_norm,
        qkv_new[0],
        qkv_new[1],
        qkv_new[2],
        out_new[0],
        out_new[1],
        out_new[2],
        up_new[0],
        up_new[1],
        up_new[2],
        down_new[0],
        down_new[1],
        down_new[2],
        norm_new[0],
        norm_new[1],
        norm_new[2],
        norm_grad,
    )


def solution(mesh):
    return jax.shard_map(
        body,
        mesh=mesh,
        in_specs=(
            P("dp", None),
            P("dp", None),
            P("dp", None),
            P("dp", None),
            P(None, "dp", "mp"),
            P("mp", "dp"),
            P("dp", "mp"),
            P("mp", "dp"),
            P(None, "dp"),
            P(None, "dp", "mp"),
            P(None, "dp", "mp"),
            P("mp", "dp"),
            P("mp", "dp"),
            P("dp", "mp"),
            P("dp", "mp"),
            P("mp", "dp"),
            P("mp", "dp"),
            P(None, "dp"),
            P(None, "dp"),
        ),
        out_specs=(
            P("dp", None),
            P("dp", None),
            P(),
            P(None, "dp", "mp"),
            P(None, "dp", "mp"),
            P(None, "dp", "mp"),
            P("mp", "dp"),
            P("mp", "dp"),
            P("mp", "dp"),
            P("dp", "mp"),
            P("dp", "mp"),
            P("dp", "mp"),
            P("mp", "dp"),
            P("mp", "dp"),
            P("mp", "dp"),
            P(None, "dp"),
            P(None, "dp"),
            P(None, "dp"),
            P(None, "dp"),
        ),
        check_vma=False,
    )
```

```python
import jax
import jax.numpy as jnp
from jax import lax
from jax.experimental import pallas as pl
from jax.experimental.pallas import tpu as pltpu
from jax.sharding import PartitionSpec as P

MESH = pl.DeviceIdType.MESH

BF = jnp.bfloat16
F32 = jnp.float32
HEAD = 64
LEN = 128
ROWS = 512
D = 768
SEQS = 4
WIDE = 384
CLIP_AT = 1.0
BETA_ONE = 0.9
BETA_TWO = 0.95
ADAM_EPS = 1e-08
STEP = 10
WEIGHT_DECAY = 0.01
RATE_MATRIX = 0.05
RATE_OUT = 0.3
RATE_VECTOR = 0.5
COPIES = 320
NORM_EPS = 1e-05


def nn(a, b):
    return jnp.dot(a, b, preferred_element_type=F32)


def nt(a, b):
    return lax.dot_general(a, b, (((1,), (1,)), ((), ())), preferred_element_type=F32)


def tn(a, b):
    return lax.dot_general(a, b, (((0,), (0,)), ((), ())), preferred_element_type=F32)


def whole(W, p, owner, zp):
    return W[p, owner, zp].reshape(D, D)


def columns(W, zp, base):
    return W[0, 1, zp, :, :, :, base : base + 256].reshape(D, 256)


def tiles(x):
    return x.astype(BF).reshape(4, 4, 48, x.shape[1])


def norm_stats(x):
    center = jnp.mean(x, axis=-1, keepdims=True)
    off = x - center
    inv = lax.rsqrt(jnp.mean(off * off, axis=-1, keepdims=True) + NORM_EPS)
    return off * inv, inv


def low_lanes(x):
    lane = lax.broadcasted_iota(jnp.int32, x.shape, x.ndim - 1)
    return lane < HEAD


def split_heads(x):
    first = low_lanes(x)
    zero = jnp.zeros_like(x)
    return jnp.concatenate([jnp.where(first, x, zero), jnp.where(first, zero, x)], axis=0)


def swap_halves(x):
    return pltpu.roll(x.astype(F32), HEAD, 1).astype(x.dtype)


def seq_rows(s):
    return pl.ds(pl.multiple_of(s * LEN, LEN), LEN)


def first_norm(place, tok, time, gains, segs, xs, n1, bias):
    for s in range(SEQS):
        rows = slice(s * LEN, s * LEN + LEN)
        x = tok[rows, :].astype(F32) + time[pl.ds(SEQS * place + s, 1), :]
        xs[rows, :] = x
        scaled, _ = norm_stats(x)
        n1[rows, :] = (scaled * gains[0:1, :] + gains[1:2, :]).astype(BF)
        lab = jnp.broadcast_to(segs[pl.ds(SEQS * place + s, 1), :].astype(F32), (LEN, LEN))
        bias[s] = jnp.where(lab == lab.T, 0.0, -1e30).astype(F32)


def project(n1, W, pq, pv):
    for zp in range(2):
        pq[zp] = nn(n1[...], whole(W, 0, 0, zp)).astype(BF)
        for j in range(2):
            pv[2 * zp + j] = nn(n1[...], columns(W, zp, 384 * j)).astype(BF)


def softmax_rows(scores):
    e = jnp.exp(scores - jnp.max(scores, axis=-1, keepdims=True))
    return e / jnp.sum(e, axis=-1, keepdims=True)


def value_two(vg):
    first = low_lanes(vg)
    return swap_halves(jnp.where(first, vg, jnp.zeros_like(vg)))


def attention(lo, hi, pq, pv, bias, probs, mx):
    scaling = HEAD ** (-0.5)

    def step(i, _):
        s, zp = i // 2, i % 2
        rows = seq_rows(s)
        mask = bias[s]
        mask2 = jnp.concatenate([mask, mask], axis=0)
        for j in range(2):
            z = 2 * zp + j
            base = 384 * j
            ga = pq[zp, rows, base : base + 128]
            gb = pq[zp, rows, base + 128 : base + 256]
            gc = pq[zp, rows, base + 256 : base + 384]
            va = pv[z, rows, 0:128]
            vb = value_two(pv[z, rows, 128:256])
            p01 = softmax_rows(nt(split_heads(ga), gc) * scaling + mask2).astype(BF)
            first = low_lanes(gb)
            p2 = softmax_rows(
                nt(jnp.where(first, gb, jnp.zeros_like(gb)), swap_halves(gb)) * scaling + mask
            ).astype(BF)
            probs[s, z, 0:256, :] = p01
            probs[s, z, 256:384, :] = p2
            m01 = nn(jnp.concatenate([p01[:LEN], p01[LEN:]], axis=1), split_heads(va))
            mx[z, rows, 128:256] = m01.astype(BF)
            mx[z, rows, 0:128] = nn(p2, vb).astype(BF)
        return 0

    lax.fori_loop(lo, hi, step, 0)


def second_norm(W, mx, xs, gains, mid, n2):
    acc = xs[...]
    for z in range(4):
        base = 384 * (z % 2) + 128
        acc = acc + nt(mx[z], columns(W, z // 2, base))
    mid[...] = acc

    def per_seq(s, _):
        rows = seq_rows(s)
        scaled, _ = norm_stats(mid[rows, :])
        n2[rows, :] = (scaled * gains[2:3, :] + gains[3:4, :]).astype(BF)
        return 0

    lax.fori_loop(0, SEQS, per_seq, 0)


def gelu_parts(u):
    cdf = 0.5 * (1.0 + lax.erf(u * 0.7071067811865476))
    pdf = jnp.exp(u * u * -0.5) * 0.3989422804014327
    return u * cdf, cdf + u * pdf


def feed_forward(p, zp, W, G, n2, ct, act, gbef, acc_out, acc_g, first):
    for h in range(2):
        rows = slice(256 * h, 256 * h + 256)
        a, slope = gelu_parts(nn(n2[rows, :], whole(W, p, 0, zp)))
        act[rows, :] = a.astype(BF)
        gbef[rows, :] = (nn(ct[rows, :], whole(W, p, 1, zp)) * slope).astype(BF)
    out = nt(act[...], whole(W, p, 1, zp))
    back = nt(gbef[...], whole(W, p, 0, zp))
    if first:
        acc_out[...] = out
        acc_g[...] = back
    else:
        acc_out[...] += out
        acc_g[...] += back
    G[p, 1, zp] = tiles(tn(ct[...], act[...]))
    G[p, 0, zp] = tiles(tn(n2[...], gbef[...]))


def norm_back(grad, scaled, inv, gain):
    u = grad * gain
    m1 = jnp.mean(u, axis=-1, keepdims=True)
    m2 = jnp.mean(u * scaled, axis=-1, keepdims=True)
    return inv * (u - m1 - scaled * m2)


def second_back(mid, acc_g, ct, gains, br, ng):
    ng[...] = jnp.zeros_like(ng)

    def per_seq(s, _):
        rows = seq_rows(s)
        scaled, inv = norm_stats(mid[rows, :])
        g = acc_g[rows, :]
        ng[2:3, :] += jnp.sum(g * scaled, axis=0, keepdims=True)
        ng[3:4, :] += jnp.sum(g, axis=0, keepdims=True)
        gm = ct[rows, :].astype(F32) + norm_back(g, scaled, inv, gains[2:3, :])
        mid[rows, :] = gm
        br[rows, :] = gm.astype(BF)
        return 0

    lax.fori_loop(0, SEQS, per_seq, 0)


def mixed_grad(W, br, dm):
    for z in range(4):
        base = 384 * (z % 2) + 128
        dm[z] = nn(br[...], columns(W, z // 2, base)).astype(BF)


def attention_back(lo, hi, pq, pv, probs, dm, dpq, dpv):
    scaling = HEAD ** (-0.5)

    def step(i, _):
        s, zp = i // 2, i % 2
        rows = seq_rows(s)
        for j in range(2):
            z = 2 * zp + j
            base = 384 * j
            ga = pq[zp, rows, base : base + 128]
            gb = pq[zp, rows, base + 128 : base + 256]
            gc = pq[zp, rows, base + 256 : base + 384]
            va = pv[z, rows, 0:128]
            vb = value_two(pv[z, rows, 128:256])
            p01 = probs[s, z, 0:256, :]
            p2 = probs[s, z, 256:384, :]
            db = dm[z, rows, 0:128]
            da = split_heads(dm[z, rows, 128:256])
            gp = nt(da, va)
            pf = p01.astype(F32)
            ds01 = (pf * (gp - jnp.sum(gp * pf, axis=-1, keepdims=True))).astype(BF)
            gp2 = nt(db, vb)
            pf2 = p2.astype(F32)
            ds2 = (pf2 * (gp2 - jnp.sum(gp2 * pf2, axis=-1, keepdims=True))).astype(BF)
            dv01 = tn(p01, da)
            dv2 = pltpu.roll(tn(p2, db), HEAD, 1)
            dk01 = tn(ds01, split_heads(ga)) * scaling
            dq01 = nn(jnp.concatenate([ds01[:LEN], ds01[LEN:]], axis=1), split_heads(gc)) * scaling
            both = swap_halves(gb)
            dq2 = nn(ds2, both)
            dk2 = tn(ds2, both)
            first = low_lanes(dq2)
            dpq[zp, rows, base : base + 128] = dq01.astype(BF)
            dpq[zp, rows, base + 128 : base + 256] = (jnp.where(first, dq2, dk2) * scaling).astype(BF)
            dpq[zp, rows, base + 256 : base + 384] = dk01.astype(BF)
            dpv[z, rows, 0:128] = dv01.astype(BF)
            dpv[z, rows, 128:256] = jnp.where(first, dv2, 0.0).astype(BF)
        return 0

    lax.fori_loop(lo, hi, step, 0)


def input_grad_sum(W, dpq, dpv, gn):
    acc = nt(dpq[0], whole(W, 0, 0, 0)) + nt(dpq[1], whole(W, 0, 0, 1))
    for z in range(4):
        acc = acc + nt(dpv[z], columns(W, z // 2, 384 * (z % 2)))
    gn[...] = acc


def first_grads(zp, G, n1, br, mx, dpq, dpv):
    G[0, 0, zp] = tiles(tn(n1[...], dpq[zp]))
    for j in range(2):
        z = 2 * zp + j
        base = 384 * j
        gv = tn(n1[...], dpv[z])
        go = tn(br[...], mx[z])
        G[0, 1, zp, :, :, :, base : base + 128] = tiles(gv[:, :128])
        G[0, 1, zp, :, :, :, base + 128 : base + 256] = tiles(gv[:, 128:] + go[:, :128])
        G[0, 1, zp, :, :, :, base + 256 : base + 384] = tiles(go[:, 128:])


def first_back(xs, gn, mid, gains, ng, dx):
    def per_seq(s, _):
        rows = seq_rows(s)
        scaled, inv = norm_stats(xs[rows, :])
        g = gn[rows, :]
        ng[0:1, :] += jnp.sum(g * scaled, axis=0, keepdims=True)
        ng[1:2, :] += jnp.sum(g, axis=0, keepdims=True)
        dx[rows, :] = (mid[rows, :] + norm_back(g, scaled, inv, gains[0:1, :])).astype(BF)
        return 0

    lax.fori_loop(0, SEQS, per_seq, 0)


class Place:
    def __init__(self):
        dp = lax.axis_index("dp")
        self.dp = dp
        self.at = {"z": lax.axis_index("mp"), "y": dp // 8, "x": (dp // 2) % 4, "c": dp % 2}

    def step(self, axis, d):
        return (self.at[axis] + d) % (2 if axis == "c" else 4)

    def device(self, axis, d):
        q = dict(self.at)
        q[axis] = self.step(axis, d)
        return ((q["y"] * 4 + q["x"]) * 2 + q["c"], q["z"])


class Net:
    def __init__(self, place, send_sem, recv_sem):
        self.place, self.send_sem, self.recv_sem = place, send_sem, recv_sem
        self.count = 0
        self.sent = []

    def push(self, src, dst, axis, d, land):
        k = self.count
        self.count += 1
        to = self.place.device(axis, d)

        def copy(target):
            return pltpu.make_async_remote_copy(
                src_ref=src,
                dst_ref=target,
                send_sem=self.send_sem.at[k],
                recv_sem=self.recv_sem.at[k],
                device_id=to,
                device_id_type=MESH,
            )

        out = copy(dst)
        out.start()
        self.sent.append(out)
        return copy(land)

    def finish(self):
        for out in self.sent:
            out.wait_send()


def arrive(copies):
    for copy in copies:
        copy.wait_recv()


def lanes(z):
    return pl.ds(pl.multiple_of((z % 2) * WIDE, 128), WIDE)


def weight_view(W, p, owner, r, at):
    y = slice(None) if at["y"] is None else at["y"]
    x = slice(None) if at["x"] is None else at["x"]
    rows = pl.ds(16 * r, 16)
    if at["z"] is None:
        return W.at[p, owner, :, y, x, rows, :]
    return W.at[p, owner, at["z"] // 2, y, x, rows, lanes(at["z"])]


ORDERS = (("x", "y", "z"), ("y", "z", "x"), ("z", "x", "y"))


class Gather:
    def __init__(self, net, W, p):
        self.net, self.W, self.p = net, W, p
        self.core = net.place.at["c"]
        self.across = []
        self.waits = {}

    def view(self, r, at, owner=None):
        return weight_view(self.W, self.p, self.core if owner is None else owner, r, at)

    def known(self, r, done, **moved):
        at = dict(self.net.place.at)
        for axis in ORDERS[r][:done]:
            at[axis] = None
        at.update(moved)
        return at

    def spread(self, r, done, ds):
        axis = ORDERS[r][done]
        src = self.view(r, self.known(r, done))
        return [
            self.net.push(
                src, src, axis, d, self.view(r, self.known(r, done, **{axis: self.net.place.step(axis, -d)}))
            )
            for d in ds
        ]

    def share(self, r, at):
        src = self.view(r, at)
        self.across.append(self.net.push(src, src, "c", 1, self.view(r, at, 1 - self.core)))

    def first(self):
        for r in range(3):
            self.waits[r] = self.spread(r, 0, (1, 3, 2))

    def second(self):
        for r in range(3):
            arrive(self.waits[r])
            self.waits[r] = self.spread(r, 1, (1, 3, 2))

    def third(self):
        for r in range(3):
            arrive(self.waits[r])
            self.waits[r] = self.spread(r, 2, (1, 3))
        for r in range(3):
            self.share(r, self.known(r, 2))

    def half(self, r, d, side):
        axis = ORDERS[r][2]
        cut = "x" if axis == "y" else "y"
        return self.known(r, 2, **{axis: self.net.place.step(axis, d), cut: pl.ds(2 * side, 2)})

    def fourth(self):
        for r in range(3):
            axis = ORDERS[r][2]
            waits = []
            for side, d in ((0, 1), (1, 3)):
                self.waits[r][side].wait_recv()
                src = self.view(r, self.half(r, -d, side))
                waits.append(self.net.push(src, src, axis, d, self.view(r, self.half(r, 2, side))))
            self.waits[r] = waits
        for r in range(3):
            axis = ORDERS[r][2]
            for d in (3, 1):
                self.share(r, self.known(r, 2, **{axis: self.net.place.step(axis, d)}))

    def fifth(self):
        for r in range(3):
            axis = ORDERS[r][2]
            arrive(self.waits[r])
            self.share(r, self.known(r, 2, **{axis: self.net.place.step(axis, 2)}))

    def last(self):
        arrive(self.across)


class Scatter:
    def __init__(self, net, G, p, zp, slot, cross, half, full, small):
        self.net, self.G, self.p, self.zp, self.slot = net, G, p, zp, slot
        self.cross, self.half, self.full, self.small = cross, half, full, small
        self.core = net.place.at["c"]

    def view(self, j, y, x):
        return (self.p, self.core, self.zp, y, x, slice(None), pl.ds(WIDE * j, WIDE))

    def block(self, j, d, cut=slice(None)):
        if j == 0:
            return self.view(0, cut, self.net.place.step("x", d))
        return self.view(1, self.net.place.step("y", d), cut)

    def own(self, j, d):
        at = self.net.place.at
        if j == 0:
            return self.view(0, self.net.place.step("y", d), at["x"])
        return self.view(1, at["y"], self.net.place.step("x", d))

    def to_core(self):
        src = self.G.at[self.p, 1 - self.core, self.zp]
        self.waits = [self.net.push(src, self.cross.at[self.slot], "c", 1, self.cross.at[self.slot])]

    def add_core(self):
        arrive(self.waits)

        def per_y(y, _):
            at = (self.p, self.core, self.zp, y)
            self.G[at] = self.G[at] + self.cross[self.slot, y]
            return 0

        lax.fori_loop(0, 4, per_y, 0)
        self.waits = []
        for j, axis in ((0, "x"), (1, "y")):
            for side, d in ((0, 1), (1, 3)):
                src = self.G.at[self.block(j, 2, pl.ds(2 * side, 2))]
                dst = self.half.at[self.p, self.zp, j, side]
                self.waits.append((j, axis, side, d, self.net.push(src, dst, axis, d, dst)))

    def add_half(self):
        waits, self.waits = self.waits, []
        for j, axis, side, d, copy in waits:
            copy.wait_recv()
            at = self.block(j, d, pl.ds(2 * side, 2))
            self.G[at] = self.G[at] + self.half[self.p, self.zp, j, side]
            dst = self.full.at[self.p, self.zp, j, side]
            self.waits.append(self.net.push(self.G.at[self.block(j, d)], dst, axis, d, dst))

    def add_full(self):
        arrive(self.waits)
        self.waits = []
        for j, axis in ((0, "y"), (1, "x")):
            at = self.block(j, 0)
            total = self.G[at].astype(F32)
            for side in range(2):
                total = total + self.full[self.p, self.zp, j, side].astype(F32)
            self.G[at] = total.astype(BF)
            for d in (1, 3, 2):
                dst = self.small.at[self.p, self.zp, j, d - 1]
                self.waits.append(self.net.push(self.G.at[self.own(j, d)], dst, axis, d, dst))

    def add_small(self):
        arrive(self.waits)
        for j in range(2):
            at = self.own(j, 0)
            total = self.G[at].astype(F32)
            for d in range(3):
                total = total + self.small[self.p, self.zp, j, d].astype(F32)
            self.G[at] = total.astype(BF)


class Deep:
    def __init__(self, net, G, p, tiny, done):
        self.net, self.G, self.p, self.tiny, self.done = net, G, p, tiny, done

    def chunk(self, d):
        at = self.net.place.at
        z = self.net.place.step("z", d)
        return (self.p, at["c"], z // 2, at["y"], at["x"], slice(None), lanes(z))

    def send(self):
        self.waits = []
        for d in (1, 3, 2):
            dst = self.tiny.at[self.p, d - 1]
            self.waits.append(self.net.push(self.G.at[self.chunk(d)], dst, "z", d, dst))

    def add(self):
        arrive(self.waits)
        total = self.G[self.chunk(0)].astype(F32)
        for d in range(3):
            total = total + self.tiny[self.p, d].astype(F32)
        self.done[self.p] = total
        return jnp.sum(total * total)


class Sum:
    def __init__(self, net, slots):
        self.net, self.slots = net, slots

    def send(self, axis, value):
        slots = self.slots[axis]
        here = self.net.place.at[axis]
        self.axis = axis
        slots[here] = value
        self.waits = [
            self.net.push(slots.at[here], slots.at[here], axis, d, slots.at[self.net.place.step(axis, -d)])
            for d in ((1,) if axis == "c" else (1, 3, 2))
        ]

    def add(self):
        arrive(self.waits)
        slots = self.slots[self.axis]
        total = slots[0]
        for k in range(1, slots.shape[0]):
            total = total + slots[k]
        return total


class Rows:
    def __init__(self, net, rows_ref, out, sem):
        self.net, self.rows_ref, self.out, self.sem = net, rows_ref, out, sem

    def place_of(self, d, piece, side=None):
        start = ROWS * self.net.place.step("z", d) + 256 * piece
        if side is None:
            return self.out.at[pl.ds(pl.multiple_of(start, 256), 256), :]
        return self.out.at[pl.ds(pl.multiple_of(start + 128 * side, 128), 128), :]

    def send(self):
        start = pl.multiple_of(ROWS * self.net.place.at["z"], ROWS)
        self.local = pltpu.make_async_copy(self.rows_ref, self.out.at[pl.ds(start, ROWS), :], self.sem)
        self.local.start()
        self.near = []
        self.far = []
        for piece in range(2):
            src = self.rows_ref.at[pl.ds(256 * piece, 256), :]
            self.near.append(
                [self.net.push(src, self.place_of(0, piece), "z", d, self.place_of(-d, piece)) for d in (1, 3)]
            )

    def forward(self, piece):
        for side, d in ((0, 1), (1, 3)):
            self.near[piece][side].wait_recv()
            src = self.place_of(-d, piece, side)
            self.far.append(self.net.push(src, src, "z", d, self.place_of(2, piece, side)))

    def finish(self):
        arrive(self.far)
        self.local.wait()


def pack(wq, wo, wu, wd, keep):
    q, k, v, o = wq[0], wq[1], wq[2], wo[...]
    keep[0, 0] = jnp.concatenate([q, k[:, 128:], k[:, :128]], axis=1)
    keep[1, 0] = jnp.concatenate([v, o[:, 128:], o[:, :128]], axis=1)
    for half in range(2):
        keep[0, 1 + half] = wu[:, WIDE * half : WIDE * half + WIDE]
        keep[1, 1 + half] = wd[:, WIDE * half : WIDE * half + WIDE]


def layer_kernel(
    tokens, time_emb, segs, cotangent, wq, wo, wu, wd, norm,
    out, input_grad, shards, norm_sum, square_sum,
    W, G, cross, half, full, small, tiny, done, keep, other,
    gx, gy, gc, nx, ny, nz, nc, sx, sy, sz, sc, gains, time, ng,
    xs, n1, bias, pq, pv, probs, mx, mid, n2, act, gbef, acc_out, acc_g, dm, dpq, dpv, tok, ct,
    send_sem, recv_sem, local_sem, free_sem,
):
    place = Place()
    net = Net(place, send_sem, recv_sem)
    z, core = place.at["z"], place.at["c"]
    mine = pl.ds(pl.multiple_of(ROWS * z, ROWS), ROWS)
    loads = [
        pltpu.make_async_copy(tokens.at[mine, :], tok, local_sem.at[0]),
        pltpu.make_async_copy(cotangent.at[mine, :], ct, local_sem.at[1]),
    ]
    for load in loads:
        load.start()
    barrier = pltpu.get_barrier_semaphore()
    for axis in ("x", "y", "z"):
        for d in (1, 2, 3):
            pl.semaphore_signal(barrier, inc=1, device_id=place.device(axis, d), device_id_type=MESH)
    pl.semaphore_signal(barrier, inc=1, device_id=place.device("c", 1), device_id_type=MESH)
    pack(wq, wo, wu, wd, keep)
    time[...] = time_emb[...].astype(F32)
    column = lax.broadcasted_iota(jnp.int32, (24, D), 1)
    row = lax.broadcasted_iota(jnp.int32, (24, D), 0)
    spot = jnp.where(column == row + 24 * place.dp, 1.0, 0.0).astype(F32)
    rounded = norm[...].astype(BF).astype(F32)
    spread = jnp.concatenate([nn(rounded, spot), jnp.zeros((4, D), F32)], axis=0)
    pl.semaphore_wait(barrier, 10)

    swap = net.push(keep.at[1 - core], other, "c", 1, other)
    gain_sum = Sum(net, {"x": gx, "y": gy, "c": gc})
    gain_sum.send("x", spread)
    swap.wait_recv()
    for p in range(3):
        kept = keep[core, p]
        came = other[p]
        even = core == 0
        rows = jnp.concatenate([jnp.where(even, kept, came), jnp.where(even, came, kept)], axis=0)
        W[p, core, z // 2, place.at["y"], place.at["x"], :, lanes(z)] = rows.astype(BF)
    parts = [Gather(net, W, p) for p in range(3)]
    for part in parts:
        part.first()
    gain_sum.send("y", gain_sum.add())
    for part in parts:
        part.second()
    gain_sum.send("c", gain_sum.add())
    parts[0].third()
    parts[1].third()
    gains[...] = gain_sum.add()
    for load in loads:
        load.wait()
    first_norm(z, tok, time, gains, segs, xs, n1, bias)
    parts[0].fourth()
    parts[2].third()
    parts[0].fifth()
    parts[0].last()

    project(n1, W, pq, pv)
    parts[1].fourth()
    attention(0, 4, pq, pv, bias, probs, mx)
    parts[1].fifth()
    parts[2].fourth()
    attention(4, 8, pq, pv, bias, probs, mx)
    second_norm(W, mx, xs, gains, mid, n2)
    parts[1].last()

    sums = {}
    for p, zp in ((1, 0), (1, 1), (2, 0), (2, 1), (0, 0), (0, 1)):
        sums[p, zp] = Scatter(net, G, p, zp, 2 * max(p - 1, 0) + zp, cross, half, full, small)
    deep = [Deep(net, G, p, tiny, done) for p in range(3)]

    def feed(p, zp):
        feed_forward(p, zp, W, G, n2, ct, act, gbef, acc_out, acc_g, p == 1 and zp == 0)
        sums[p, zp].to_core()

    def free():
        pl.semaphore_signal(free_sem, inc=1, device_id=place.device("c", 1), device_id_type=MESH)

    feed(1, 0)
    parts[2].fifth()
    feed(1, 1)
    sums[1, 0].add_core()
    free()
    parts[2].last()
    feed(2, 0)
    sums[1, 1].add_core()
    free()
    sums[1, 0].add_half()
    feed(2, 1)
    sums[2, 0].add_core()
    tok[...] = (mid[...] + acc_out[...]).astype(BF)
    out_rows = Rows(net, tok, out, local_sem.at[2])
    out_rows.send()
    sums[1, 1].add_half()
    sums[1, 0].add_full()
    second_back(mid, acc_g, ct, gains, act, ng)
    br = act
    sums[2, 1].add_core()
    sums[2, 0].add_half()
    sums[1, 1].add_full()
    mixed_grad(W, br, dm)
    sums[1, 0].add_small()
    attention_back(0, 4, pq, pv, probs, dm, dpq, dpv)
    sums[2, 1].add_half()
    sums[2, 0].add_full()
    sums[1, 1].add_small()
    deep[1].send()
    out_rows.forward(0)
    attention_back(4, 8, pq, pv, probs, dm, dpq, dpv)
    sums[2, 1].add_full()
    sums[2, 0].add_small()
    out_rows.forward(1)
    input_grad_sum(W, dpq, dpv, acc_g)
    first_back(xs, acc_g, mid, gains, ng, n2)
    in_rows = Rows(net, n2, input_grad, local_sem.at[3])
    in_rows.send()
    norm_total = Sum(net, {"c": nc, "x": nx, "y": ny, "z": nz})
    norm_total.send("c", ng[...])
    pl.semaphore_wait(free_sem, 2)
    first_grads(0, G, n1, br, mx, dpq, dpv)
    sums[0, 0].to_core()
    sums[2, 1].add_small()
    deep[2].send()
    first_grads(1, G, n1, br, mx, dpq, dpv)
    sums[0, 1].to_core()
    norm_total.send("x", norm_total.add())
    sums[0, 0].add_core()
    sums[0, 1].add_core()
    squares = deep[1].add() + deep[2].add()
    norm_total.send("y", norm_total.add())
    sums[0, 0].add_half()
    sums[0, 1].add_half()
    norm_total.send("z", norm_total.add())
    sums[0, 0].add_full()
    sums[0, 1].add_full()
    in_rows.forward(0)
    in_rows.forward(1)
    sums[0, 0].add_small()
    sums[0, 1].add_small()
    deep[0].send()
    norm_rows = norm_total.add()
    norm_sum[...] = norm_rows
    squares = squares + deep[0].add()
    other_rows = pl.ds(pl.multiple_of(24 * (1 - core), 8), 24)
    own_rows = pl.ds(pl.multiple_of(24 * core, 8), 24)
    trade = net.push(done.at[:, other_rows, :], shards.at[core], "c", 1, shards.at[1 - core])
    shards[core] = done[:, own_rows, :]
    total = Sum(net, {"c": sc, "x": sx, "y": sy, "z": sz})
    total.send("c", jnp.full((8, 128), squares, F32))
    total.send("x", total.add())
    total.send("y", total.add())
    total.send("z", total.add())
    square_sum[...] = total.add() + jnp.sum(norm_rows * norm_rows)
    trade.wait_recv()
    out_rows.finish()
    in_rows.finish()
    net.finish()


def layer(tokens, time_emb, segs, cotangent, wq, wo, wu, wd, norm):
    V = pltpu.VMEM
    rows, low = (ROWS, D), BF
    anywhere = pl.BlockSpec(memory_space=pl.ANY)
    near = pl.BlockSpec(memory_space=pltpu.VMEM)
    return pl.pallas_call(
        layer_kernel,
        name="layer",
        out_shape=(
            jax.ShapeDtypeStruct(tokens.shape, BF),
            jax.ShapeDtypeStruct(tokens.shape, BF),
            jax.ShapeDtypeStruct((2, 3, 24, WIDE), F32),
            jax.ShapeDtypeStruct((8, D), F32),
            jax.ShapeDtypeStruct((8, 128), F32),
        ),
        in_specs=[anywhere, near, near, anywhere] + [near] * 5,
        out_specs=[anywhere, anywhere, near, near, near],
        scratch_shapes=[
            V((3, 2, 2, 4, 4, 48, D), low),
            V((3, 2, 2, 4, 4, 48, D), low),
            V((4, 4, 4, 48, D), low),
            V((3, 2, 2, 2, 2, 48, WIDE), low),
            V((3, 2, 2, 2, 4, 48, WIDE), low),
            V((3, 2, 2, 3, 48, WIDE), low),
            V((3, 3, 48, WIDE), low),
            V((3, 48, WIDE), F32),
            V((2, 3, 24, WIDE), F32),
            V((3, 24, WIDE), F32),
            V((4, 8, D), F32),
            V((4, 8, D), F32),
            V((2, 8, D), F32),
            V((4, 8, D), F32),
            V((4, 8, D), F32),
            V((4, 8, D), F32),
            V((2, 8, D), F32),
            V((4, 8, 128), F32),
            V((4, 8, 128), F32),
            V((4, 8, 128), F32),
            V((2, 8, 128), F32),
            V((8, D), F32),
            V((16, D), F32),
            V((8, D), F32),
            V(rows, F32),
            V(rows, low),
            V((SEQS, LEN, LEN), F32),
            V((2, ROWS, D), low),
            V((4, ROWS, 256), low),
            V((SEQS, 4, WIDE, LEN), low),
            V((4, ROWS, 256), low),
            V(rows, F32),
            V(rows, low),
            V(rows, low),
            V(rows, low),
            V(rows, F32),
            V(rows, F32),
            V((4, ROWS, 256), low),
            V((2, ROWS, D), low),
            V((4, ROWS, 256), low),
            V(rows, low),
            V(rows, low),
            pltpu.SemaphoreType.DMA((COPIES,)),
            pltpu.SemaphoreType.DMA((COPIES,)),
            pltpu.SemaphoreType.DMA((4,)),
            pltpu.SemaphoreType.REGULAR,
        ],
        compiler_params=pltpu.CompilerParams(
            collective_id=0, has_side_effects=True, vmem_limit_bytes=64 * 2**20
        ),
    )(tokens, time_emb, segs, cotangent, wq, wo, wu, wd, norm)


def adam(weight, gradient, moment, second, step_rate, decay_rate):
    moment = BETA_ONE * moment + (1.0 - BETA_ONE) * gradient
    second = BETA_TWO * second + (1.0 - BETA_TWO) * gradient * gradient
    moment_hat = moment / (1.0 - BETA_ONE**STEP)
    second_hat = second / (1.0 - BETA_TWO**STEP)
    weight = weight - step_rate * (
        moment_hat / (jnp.sqrt(second_hat) + ADAM_EPS) + decay_rate * weight
    )
    return (moment, second, weight)


def step_kernel(
    out_in, grad_in, shards, norm_sum, square_sum, wq, wo, wu, wd, norm,
    qm, qs, om, os, um, us, dm, ds, nm, ns,
    out, grad, total, qm_new, qs_new, q_new, om_new, os_new, o_new, um_new, us_new, u_new, dm_new, ds_new, d_new,
    nm_new, ns_new, n_new, norm_grad, sem,
):
    copies = [
        pltpu.make_async_copy(out_in, out, sem.at[0]),
        pltpu.make_async_copy(grad_in, grad, sem.at[1]),
    ]
    for copy in copies:
        copy.start()
    grad_norm = jnp.sqrt(square_sum[0:1, 0:1])
    total[...] = grad_norm
    factor = jnp.minimum(1.0, CLIP_AT / (grad_norm + 1e-06))

    def put(refs, at, value):
        for ref, new in zip(refs, value):
            ref[at] = new

    first, second = shards[0, 0], shards[1, 0]
    tail = lambda v: jnp.concatenate([v[:, 256:], v[:, 192:256]], axis=1)
    for c, g in enumerate((first[:, :192], tail(first), second[:, :192])):
        put((qm_new, qs_new, q_new), c, adam(wq[c], g * factor, qm[c], qs[c], RATE_MATRIX, WEIGHT_DECAY))
    put((om_new, os_new, o_new), ..., adam(wo[...], tail(second) * factor, om[...], os[...], RATE_OUT, WEIGHT_DECAY))
    for half in range(2):
        at = (slice(None), pl.ds(WIDE * half, WIDE))
        g = shards[0, 1 + half] * factor
        put((um_new, us_new, u_new), at, adam(wu[at], g, um[at], us[at], RATE_MATRIX, WEIGHT_DECAY))
        g = shards[1, 1 + half] * factor
        put((dm_new, ds_new, d_new), at, adam(wd[at], g, dm[at], ds[at], RATE_MATRIX, WEIGHT_DECAY))
    start = lax.axis_index("dp") * 24
    rolled = pltpu.roll(norm_sum[...], lax.rem(D - start, D), 1)
    g = rolled[0:4, 0:24] * factor
    norm_grad[...] = g
    put((nm_new, ns_new, n_new), ..., adam(norm[...], g, nm[...], ns[...], RATE_VECTOR, 0.0))
    for copy in copies:
        copy.wait()


def step(out_in, grad_in, shards, norm_sum, square_sum, weights, moments):
    anywhere = pl.BlockSpec(memory_space=pl.ANY)
    near = pl.BlockSpec(memory_space=pltpu.VMEM)
    like = lambda v: jax.ShapeDtypeStruct(v.shape, v.dtype)
    shapes = [like(out_in), like(grad_in), jax.ShapeDtypeStruct((1, 1), F32)]
    for w in weights:
        shapes += [like(w)] * 3
    shapes.append(like(weights[-1]))
    return pl.pallas_call(
        step_kernel,
        name="step",
        out_shape=shapes,
        in_specs=[anywhere] * 2 + [near] * (3 + len(weights) + len(moments)),
        out_specs=[anywhere] * 2 + [near] * (len(shapes) - 2),
        scratch_shapes=[pltpu.SemaphoreType.DMA((2,))],
        compiler_params=pltpu.CompilerParams(vmem_limit_bytes=32 * 2**20),
    )(out_in, grad_in, shards, norm_sum, square_sum, *weights, *moments)


def body(
    tokens, time_emb, segments, cotangent, w_qkv, w_out, w_up, w_down, norm_params,
    qkv_first, qkv_second, out_first, out_second, up_first, up_second, down_first, down_second, norm_first, norm_second,
):
    weights = (w_qkv, w_out.T, w_up, w_down.T, norm_params)
    sent = layer(tokens, time_emb, segments, cotangent, *weights)
    moments = (
        qkv_first, qkv_second, out_first.T, out_second.T, up_first, up_second, down_first.T, down_second.T,
        norm_first, norm_second,
    )
    new = list(step(*sent, weights, moments))
    new[2] = new[2].reshape(())
    for k in (6, 7, 8, 12, 13, 14):
        new[k] = new[k].T
    return tuple(new)


def solution(mesh):
    return jax.shard_map(
        body,
        mesh=mesh,
        in_specs=(
            P("dp", None),
            P("dp", None),
            P("dp", None),
            P("dp", None),
            P(None, "dp", "mp"),
            P("mp", "dp"),
            P("dp", "mp"),
            P("mp", "dp"),
            P(None, "dp"),
            P(None, "dp", "mp"),
            P(None, "dp", "mp"),
            P("mp", "dp"),
            P("mp", "dp"),
            P("dp", "mp"),
            P("dp", "mp"),
            P("mp", "dp"),
            P("mp", "dp"),
            P(None, "dp"),
            P(None, "dp"),
        ),
        out_specs=(
            P("dp", None),
            P("dp", None),
            P(),
            P(None, "dp", "mp"),
            P(None, "dp", "mp"),
            P(None, "dp", "mp"),
            P("mp", "dp"),
            P("mp", "dp"),
            P("mp", "dp"),
            P("dp", "mp"),
            P("dp", "mp"),
            P("dp", "mp"),
            P("mp", "dp"),
            P("mp", "dp"),
            P("mp", "dp"),
            P(None, "dp"),
            P(None, "dp"),
            P(None, "dp"),
            P(None, "dp"),
        ),
        check_vma=False,
    )
```

```python
import jax
import jax.numpy as jnp
from jax import lax
from jax.experimental import pallas as pl
from jax.experimental.pallas import tpu as pltpu
from jax.sharding import PartitionSpec as P

MESH = pl.DeviceIdType.MESH

BF = jnp.bfloat16
F32 = jnp.float32
HEAD = 64
LEN = 128
ROWS = 512
D = 768
SEQS = 4
WIDE = 384
CLIP_AT = 1.0
BETA_ONE = 0.9
BETA_TWO = 0.95
ADAM_EPS = 1e-08
STEP = 10
WEIGHT_DECAY = 0.01
RATE_MATRIX = 0.05
RATE_OUT = 0.3
RATE_VECTOR = 0.5
GROUPS = 64
NORM_EPS = 1e-05


def nn(a, b):
    return jnp.dot(a, b, preferred_element_type=F32)


def nt(a, b):
    return lax.dot_general(a, b, (((1,), (1,)), ((), ())), preferred_element_type=F32)


def tn(a, b):
    return lax.dot_general(a, b, (((0,), (0,)), ((), ())), preferred_element_type=F32)


def whole(W, p, owner, zp):
    return W[p, owner, zp].reshape(D, D)


def columns(W, zp, base):
    return W[0, 1, zp, :, :, :, base : base + 256].reshape(D, 256)


def tiles(x):
    return x.astype(BF).reshape(4, 4, 48, x.shape[1])


def norm_stats(x):
    center = jnp.mean(x, axis=-1, keepdims=True)
    off = x - center
    inv = lax.rsqrt(jnp.mean(off * off, axis=-1, keepdims=True) + NORM_EPS)
    return off * inv, inv


def low_lanes(x):
    lane = lax.broadcasted_iota(jnp.int32, x.shape, x.ndim - 1)
    return lane < HEAD


def split_heads(x):
    first = low_lanes(x)
    zero = jnp.zeros_like(x)
    return jnp.concatenate([jnp.where(first, x, zero), jnp.where(first, zero, x)], axis=0)


def swap_halves(x):
    return pltpu.roll(x.astype(F32), HEAD, 1).astype(x.dtype)


def seq_rows(s):
    return pl.ds(pl.multiple_of(s * LEN, LEN), LEN)


def first_norm(place, tok, time, gains, segs, xs, n1, bias):
    for s in range(SEQS):
        rows = slice(s * LEN, s * LEN + LEN)
        x = tok[rows, :].astype(F32) + time[pl.ds(SEQS * place + s, 1), :]
        xs[rows, :] = x
        scaled, _ = norm_stats(x)
        n1[rows, :] = (scaled * gains[0:1, :] + gains[1:2, :]).astype(BF)
        lab = jnp.broadcast_to(segs[pl.ds(SEQS * place + s, 1), :].astype(F32), (LEN, LEN))
        bias[s] = jnp.where(lab == lab.T, 0.0, -1e30).astype(F32)


def project(n1, W, pq, pv):
    for zp in range(2):
        pq[zp] = nn(n1[...], whole(W, 0, 0, zp)).astype(BF)
        for j in range(2):
            pv[2 * zp + j] = nn(n1[...], columns(W, zp, 384 * j)).astype(BF)


def softmax_columns(scores):
    e = jnp.exp(scores - jnp.max(scores, axis=1, keepdims=True))
    return (e * (1.0 / jnp.sum(e, axis=1, keepdims=True))).astype(BF)


def value_two(vg):
    first = low_lanes(vg)
    return swap_halves(jnp.where(first, vg, jnp.zeros_like(vg)))


def attention(lo, hi, pq, pv, bias, probs, mx):
    scaling = HEAD ** (-0.5)

    def step(i, _):
        s, zp = i // 2, i % 2
        rows = seq_rows(s)
        mask = bias[s]
        for j in range(2):
            z = 2 * zp + j
            base = 384 * j
            ga = pq[zp, rows, base : base + 128]
            gb = pq[zp, rows, base + 128 : base + 256]
            gc = pq[zp, rows, base + 256 : base + 384]
            va = pv[z, rows, 0:128]
            vb = value_two(pv[z, rows, 128:256])
            both = swap_halves(gb)
            first = low_lanes(gb)
            s01 = nt(split_heads(gc), ga)
            s2 = nt(jnp.where(first, both, jnp.zeros_like(gb)), gb)
            scores = jnp.concatenate([s01, s2], axis=0).reshape(3, LEN, LEN)
            p = softmax_columns(scores * scaling + mask[None]).reshape(3 * LEN, LEN)
            probs[s, z] = p
            mx[z, rows, 128:256] = tn(p[: 2 * LEN], split_heads(va)).astype(BF)
            mx[z, rows, 0:128] = tn(p[2 * LEN :], vb).astype(BF)
        return 0

    lax.fori_loop(lo, hi, step, 0, unroll=4)


def second_norm(W, mx, xs, gains, mid, n2):
    acc = xs[...]
    for z in range(4):
        base = 384 * (z % 2) + 128
        acc = acc + nt(mx[z], columns(W, z // 2, base))
    mid[...] = acc

    scaled, _ = norm_stats(mid[...])
    n2[...] = (scaled * gains[2:3, :] + gains[3:4, :]).astype(BF)


def gelu_parts(u):
    cdf = 0.5 * (1.0 + lax.erf(u * 0.7071067811865476))
    pdf = jnp.exp(u * u * -0.5) * 0.3989422804014327
    return u * cdf, cdf + u * pdf


def feed_out(p, zp, W, n2, act, slope, acc_out, first):
    at = 2 * (p - 1) + zp
    for h in range(2):
        rows = slice(256 * h, 256 * h + 256)
        a, rate = gelu_parts(nn(n2[rows, :], whole(W, p, 0, zp)))
        act[at, rows, :] = a.astype(BF)
        slope[at, rows, :] = rate.astype(BF)
    out = nt(act[at], whole(W, p, 1, zp))
    if first:
        acc_out[...] = out
    else:
        acc_out[...] += out


def feed_back(p, zp, W, G, n2, ct, act, slope, acc_g, first):
    at = 2 * (p - 1) + zp
    for h in range(2):
        rows = slice(256 * h, 256 * h + 256)
        slope[at, rows, :] = (nn(ct[rows, :], whole(W, p, 1, zp)) * slope[at, rows, :].astype(F32)).astype(BF)
    back = nt(slope[at], whole(W, p, 0, zp))
    if first:
        acc_g[...] = back
    else:
        acc_g[...] += back
    G[p, 1, zp] = tiles(tn(ct[...], act[at]))
    G[p, 0, zp] = tiles(tn(n2[...], slope[at]))


def norm_back(grad, scaled, inv, gain):
    u = grad * gain
    m1 = jnp.mean(u, axis=-1, keepdims=True)
    m2 = jnp.mean(u * scaled, axis=-1, keepdims=True)
    return inv * (u - m1 - scaled * m2)


def second_back(mid, acc_g, ct, gains, br, ng):
    ng[4:8, :] = jnp.zeros((4, D), F32)
    scaled, inv = norm_stats(mid[...])
    g = acc_g[...]
    ng[2:3, :] = jnp.sum(g * scaled, axis=0, keepdims=True)
    ng[3:4, :] = jnp.sum(g, axis=0, keepdims=True)
    gm = ct[...].astype(F32) + norm_back(g, scaled, inv, gains[2:3, :])
    mid[...] = gm
    br[...] = gm.astype(BF)


def mixed_grad(W, br, dm):
    for z in range(4):
        base = 384 * (z % 2) + 128
        dm[z // 2, :, base - 128 : base + 128] = nn(br[...], columns(W, z // 2, base)).astype(BF)


def attention_back(zp, pq, pv, probs, dm, dpq, dpv):
    scaling = HEAD ** (-0.5)

    def step(s, _):
        rows = seq_rows(s)
        for j in range(2):
            z = 2 * zp + j
            base = 384 * j
            ga = pq[zp, rows, base : base + 128]
            gb = pq[zp, rows, base + 128 : base + 256]
            gc = pq[zp, rows, base + 256 : base + 384]
            va = pv[z, rows, 0:128]
            vb = value_two(pv[z, rows, 128:256])
            p = probs[s, z]
            db = dm[zp, rows, base : base + 128]
            da = dm[zp, rows, base + 128 : base + 256]
            gp = jnp.concatenate([nt(split_heads(va), da), nt(vb, db)], axis=0).reshape(3, LEN, LEN)
            pf = p.astype(F32).reshape(3, LEN, LEN)
            ds = (pf * (gp - jnp.sum(gp * pf, axis=1, keepdims=True))).astype(BF).reshape(3 * LEN, LEN)
            beside = lambda v: jnp.concatenate([v[:LEN], v[LEN : 2 * LEN]], axis=1)
            dv01 = nn(beside(p), split_heads(da))
            dk01 = nn(beside(ds), split_heads(ga)) * scaling
            dq01 = tn(ds[: 2 * LEN], split_heads(gc)) * scaling
            dv2 = pltpu.roll(nn(p[2 * LEN :], db), HEAD, 1)
            both = swap_halves(gb)
            dk2 = nn(ds[2 * LEN :], both)
            dq2 = tn(ds[2 * LEN :], both)
            first = low_lanes(dq2)
            dpq[zp, rows, base : base + 128] = dq01.astype(BF)
            dpq[zp, rows, base + 128 : base + 256] = (jnp.where(first, dq2, dk2) * scaling).astype(BF)
            dpq[zp, rows, base + 256 : base + 384] = dk01.astype(BF)
            dpv[z, rows, 0:128] = dv01.astype(BF)
            dpv[z, rows, 128:256] = jnp.where(first, dv2, 0.0).astype(BF)
        return 0

    lax.fori_loop(0, SEQS, step, 0, unroll=4)


def input_grad_sum(W, dpq, dpv, gn):
    acc = nt(dpq[0], whole(W, 0, 0, 0)) + nt(dpq[1], whole(W, 0, 0, 1))
    for z in range(4):
        acc = acc + nt(dpv[z], columns(W, z // 2, 384 * (z % 2)))
    gn[...] = acc


def first_grads(zp, G, n1, br, mx, dpq, dpv):
    G[0, 0, zp] = tiles(tn(n1[...], dpq[zp]))
    for j in range(2):
        z = 2 * zp + j
        base = 384 * j
        gv = tn(n1[...], dpv[z])
        go = tn(br[...], mx[z])
        G[0, 1, zp, :, :, :, base : base + 128] = tiles(gv[:, :128])
        G[0, 1, zp, :, :, :, base + 128 : base + 256] = tiles(gv[:, 128:] + go[:, :128])
        G[0, 1, zp, :, :, :, base + 256 : base + 384] = tiles(go[:, 128:])


def first_back(xs, gn, mid, gains, ng, dx):
    scaled, inv = norm_stats(xs[...])
    g = gn[...]
    ng[0:1, :] = jnp.sum(g * scaled, axis=0, keepdims=True)
    ng[1:2, :] = jnp.sum(g, axis=0, keepdims=True)
    dx[...] = (mid[...] + norm_back(g, scaled, inv, gains[0:1, :])).astype(BF)


class Place:
    def __init__(self):
        dp = lax.axis_index("dp")
        self.dp = dp
        self.at = {"z": lax.axis_index("mp"), "y": dp // 8, "x": (dp // 2) % 4, "c": dp % 2}

    def step(self, axis, d):
        return (self.at[axis] + d) % (2 if axis == "c" else 4)

    def device(self, axis, d):
        q = dict(self.at)
        q[axis] = self.step(axis, d)
        return ((q["y"] * 4 + q["x"]) * 2 + q["c"], q["z"])


class Net:
    def __init__(self, place, send_sem, recv_sem):
        self.place, self.send_sem, self.recv_sem = place, send_sem, recv_sem
        self.groups = []

    def group(self, like):
        group = Group(self, len(self.groups), like)
        self.groups.append(group)
        return group

    def finish(self):
        for group in self.groups:
            group.every.wait_send()


class Group:
    def __init__(self, net, k, like):
        self.net, self.k = net, k
        self.every = self.copy(like, like, net.place.device("c", 1))

    def copy(self, src, dst, to):
        return pltpu.make_async_remote_copy(
            src_ref=src,
            dst_ref=dst,
            send_sem=self.net.send_sem.at[self.k],
            recv_sem=self.net.recv_sem.at[self.k],
            device_id=to,
            device_id_type=MESH,
        )

    def push(self, src, dst, axis, d):
        self.copy(src, dst, self.net.place.device(axis, d)).start()

    def arrive(self):
        self.every.wait_recv()


def lanes(z):
    return pl.ds(pl.multiple_of((z % 2) * WIDE, 128), WIDE)


def weight_view(W, p, owner, r, at):
    y = slice(None) if at["y"] is None else at["y"]
    x = slice(None) if at["x"] is None else at["x"]
    rows = pl.ds(16 * r, 16)
    if at["z"] is None:
        return W.at[p, owner, :, y, x, rows, :]
    return W.at[p, owner, at["z"] // 2, y, x, rows, lanes(at["z"])]


ORDERS = (("x", "y", "z"), ("y", "z", "x"), ("z", "x", "y"))


class Gather:
    def __init__(self, net, W, p):
        self.net, self.W, self.p = net, W, p
        self.core = net.place.at["c"]
        self.across = net.group(W.at[p, self.core])

    def view(self, r, at):
        return weight_view(self.W, self.p, self.core, r, at)

    def known(self, r, done, **moved):
        at = dict(self.net.place.at)
        for axis in ORDERS[r][:done]:
            at[axis] = None
        at.update(moved)
        return at

    def spread(self, done, ds, like):
        self.step = self.net.group(like)
        for r in range(3):
            src = self.view(r, self.known(r, done))
            for d in ds:
                self.step.push(src, src, ORDERS[r][done], d)

    def share(self, r, at):
        src = self.view(r, at)
        self.across.push(src, src, "c", 1)

    def first(self):
        self.spread(0, (1, 3, 2), self.W.at[self.p, self.core, 0, 0, 0:3, :, 0:WIDE])

    def second(self):
        self.step.arrive()
        self.spread(1, (1, 3, 2), self.W.at[self.p, self.core, 0, :, 0:3, :, 0:WIDE])

    def third(self):
        self.step.arrive()
        self.spread(2, (1, 3), self.W.at[self.p, self.core, 0])
        for r in range(3):
            self.share(r, self.known(r, 2))

    def fourth(self):
        self.step.arrive()
        self.step = self.net.group(self.W.at[self.p, self.core, 0, :, :, :, 0:WIDE])
        for r in range(3):
            axis = ORDERS[r][2]
            cut = "x" if axis == "y" else "y"
            for side, d in ((0, 1), (1, 3)):
                half = {axis: self.net.place.step(axis, -d), cut: pl.ds(2 * side, 2)}
                src = self.view(r, self.known(r, 2, **half))
                self.step.push(src, src, axis, d)
        for r in range(3):
            axis = ORDERS[r][2]
            for d in (3, 1):
                self.share(r, self.known(r, 2, **{axis: self.net.place.step(axis, d)}))

    def fifth(self):
        self.step.arrive()
        for r in range(3):
            axis = ORDERS[r][2]
            self.share(r, self.known(r, 2, **{axis: self.net.place.step(axis, 2)}))

    def last(self):
        self.across.arrive()


class Scatter:
    def __init__(self, net, G, p, zp, slot, cross, half, full, small):
        self.net, self.G, self.p, self.zp, self.slot = net, G, p, zp, slot
        self.cross, self.half, self.full, self.small = cross, half, full, small
        self.core = net.place.at["c"]

    def view(self, j, y, x):
        return (self.p, self.core, self.zp, y, x, slice(None), pl.ds(WIDE * j, WIDE))

    def block(self, j, d, cut=slice(None)):
        if j == 0:
            return self.view(0, cut, self.net.place.step("x", d))
        return self.view(1, self.net.place.step("y", d), cut)

    def own(self, j, d):
        at = self.net.place.at
        if j == 0:
            return self.view(0, self.net.place.step("y", d), at["x"])
        return self.view(1, at["y"], self.net.place.step("x", d))

    def to_core(self):
        dst = self.cross.at[self.slot]
        self.step = self.net.group(dst)
        self.step.push(self.G.at[self.p, 1 - self.core, self.zp], dst, "c", 1)

    def add_core(self):
        self.step.arrive()

        def per_y(y, _):
            at = (self.p, self.core, self.zp, y)
            self.G[at] = self.G[at] + self.cross[self.slot, y]
            return 0

        lax.fori_loop(0, 4, per_y, 0)
        self.step = self.net.group(self.half.at[self.p, self.zp])
        for side, d in ((0, 1), (1, 3)):
            for j, axis in ((0, "x"), (1, "y")):
                src = self.G.at[self.block(j, 2, pl.ds(2 * side, 2))]
                self.step.push(src, self.half.at[self.p, self.zp, j, side], axis, d)

    def add_half(self):
        self.step.arrive()
        self.step = self.net.group(self.full.at[self.p, self.zp])
        for side, d in ((0, 1), (1, 3)):
            for j, axis in ((0, "x"), (1, "y")):
                at = self.block(j, d, pl.ds(2 * side, 2))
                self.G[at] = self.G[at] + self.half[self.p, self.zp, j, side]
                self.step.push(self.G.at[self.block(j, d)], self.full.at[self.p, self.zp, j, side], axis, d)

    def add_full(self):
        self.step.arrive()
        self.step = self.net.group(self.small.at[self.p, self.zp])
        for j, axis in ((0, "y"), (1, "x")):
            at = self.block(j, 0)
            total = self.G[at].astype(F32)
            for side in range(2):
                total = total + self.full[self.p, self.zp, j, side].astype(F32)
            self.G[at] = total.astype(BF)
            for d in (1, 3, 2):
                self.step.push(self.G.at[self.own(j, d)], self.small.at[self.p, self.zp, j, d - 1], axis, d)

    def add_small(self):
        self.step.arrive()
        for j in range(2):
            at = self.own(j, 0)
            total = self.G[at].astype(F32)
            for d in range(3):
                total = total + self.small[self.p, self.zp, j, d].astype(F32)
            self.G[at] = total.astype(BF)


class Deep:
    def __init__(self, net, G, p, tiny, done):
        self.net, self.G, self.p, self.tiny, self.done = net, G, p, tiny, done

    def chunk(self, d):
        at = self.net.place.at
        z = self.net.place.step("z", d)
        return (self.p, at["c"], z // 2, at["y"], at["x"], slice(None), lanes(z))

    def send(self):
        self.step = self.net.group(self.tiny.at[self.p])
        for d in (1, 3, 2):
            self.step.push(self.G.at[self.chunk(d)], self.tiny.at[self.p, d - 1], "z", d)

    def add(self):
        self.step.arrive()
        total = self.G[self.chunk(0)].astype(F32)
        for d in range(3):
            total = total + self.tiny[self.p, d].astype(F32)
        self.done[self.p] = total
        return jnp.sum(total * total)


class Sum:
    def __init__(self, net, slots):
        self.net, self.slots = net, slots

    def send(self, axis, value):
        slots = self.slots[axis]
        here = self.net.place.at[axis]
        self.axis = axis
        slots[here] = value
        ds = (1,) if axis == "c" else (1, 3, 2)
        self.step = self.net.group(slots.at[0 : len(ds)])
        for d in ds:
            self.step.push(slots.at[here], slots.at[here], axis, d)

    def add(self):
        self.step.arrive()
        slots = self.slots[self.axis]
        total = slots[0]
        for k in range(1, slots.shape[0]):
            total = total + slots[k]
        return total


class Rows:
    def __init__(self, net, rows_ref, out, sem):
        self.net, self.rows_ref, self.out, self.sem = net, rows_ref, out, sem
        self.far = net.group(out.at[0:ROWS, :])

    def place_of(self, d, piece, side=None):
        start = ROWS * self.net.place.step("z", d) + 256 * piece
        if side is None:
            return self.out.at[pl.ds(pl.multiple_of(start, 256), 256), :]
        return self.out.at[pl.ds(pl.multiple_of(start + 128 * side, 128), 128), :]

    def send(self):
        start = pl.multiple_of(ROWS * self.net.place.at["z"], ROWS)
        self.local = pltpu.make_async_copy(self.rows_ref, self.out.at[pl.ds(start, ROWS), :], self.sem)
        self.local.start()
        self.near = []
        for piece in range(2):
            src = self.rows_ref.at[pl.ds(256 * piece, 256), :]
            self.near.append(self.net.group(self.out.at[0:ROWS, :]))
            for d in (1, 3):
                self.near[piece].push(src, self.place_of(0, piece), "z", d)

    def forward(self, piece):
        self.near[piece].arrive()
        for side, d in ((0, 1), (1, 3)):
            src = self.place_of(-d, piece, side)
            self.far.push(src, src, "z", d)

    def finish(self):
        self.far.arrive()
        self.local.wait()


def pack(wq, wo, wu, wd, keep):
    q, k, v, o = wq[0], wq[1], wq[2], wo[...]
    keep[0, 0] = jnp.concatenate([q, k[:, 128:], k[:, :128]], axis=1)
    keep[1, 0] = jnp.concatenate([v, o[:, 128:], o[:, :128]], axis=1)
    for half in range(2):
        keep[0, 1 + half] = wu[:, WIDE * half : WIDE * half + WIDE]
        keep[1, 1 + half] = wd[:, WIDE * half : WIDE * half + WIDE]


def layer_kernel(
    tokens, time_in, segs_in, cotangent, wq_in, wo_in, wu_in, wd_in, norm_in,
    out, input_grad, shards, norm_sum, square_sum,
    W, G, cross, half, full, small, tiny, done, keep, other,
    gx, gy, gc, nx, ny, nz, nc, sx, sy, sz, sc, gains, time, ng,
    xs, n1, bias, pq, pv, probs, mx, mid, n2, act, slope, acc_out, acc_g, br, dpv, tok, ct,
    time_emb, segs, wq, wo, wu, wd, norm,
    send_sem, recv_sem, local_sem, free_sem,
):
    place = Place()
    net = Net(place, send_sem, recv_sem)
    z, core = place.at["z"], place.at["c"]
    mine = pl.ds(pl.multiple_of(ROWS * z, ROWS), ROWS)
    pairs = (
        (wq_in, wq), (wo_in, wo), (wu_in, wu), (wd_in, wd), (norm_in, norm),
        (time_in, time_emb), (segs_in, segs), (tokens.at[mine, :], tok), (cotangent.at[mine, :], ct),
    )
    loads = [pltpu.make_async_copy(src, dst, local_sem.at[i]) for i, (src, dst) in enumerate(pairs)]
    for load in loads:
        load.start()
    barrier = pltpu.get_barrier_semaphore()
    for axis in ("x", "y", "z"):
        for d in (1, 2, 3):
            pl.semaphore_signal(barrier, inc=1, device_id=place.device(axis, d), device_id_type=MESH)
    pl.semaphore_signal(barrier, inc=1, device_id=place.device("c", 1), device_id_type=MESH)
    for load in loads[:5]:
        load.wait()
    pack(wq, wo, wu, wd, keep)
    column = lax.broadcasted_iota(jnp.int32, (24, D), 1)
    row = lax.broadcasted_iota(jnp.int32, (24, D), 0)
    spot = jnp.where(column == row + 24 * place.dp, 1.0, 0.0).astype(F32)
    rounded = norm[...].astype(BF).astype(F32)
    spread = jnp.concatenate([nn(rounded, spot), jnp.zeros((4, D), F32)], axis=0)
    pl.semaphore_wait(barrier, 10)

    swap = net.group(other)
    swap.push(keep.at[1 - core], other, "c", 1)
    gain_sum = Sum(net, {"x": gx, "y": gy, "c": gc})
    gain_sum.send("x", spread)
    swap.arrive()
    for p in range(3):
        kept = keep[core, p]
        came = other[p]
        even = core == 0
        rows = jnp.concatenate([jnp.where(even, kept, came), jnp.where(even, came, kept)], axis=0)
        W[p, core, z // 2, place.at["y"], place.at["x"], :, lanes(z)] = rows.astype(BF)
    parts = [Gather(net, W, p) for p in range(3)]
    for part in parts:
        part.first()
    gain_sum.send("y", gain_sum.add())
    parts[0].second()
    parts[1].second()
    gain_sum.send("c", gain_sum.add())
    parts[0].third()
    parts[2].second()
    for load in loads[5:]:
        load.wait()
    time[...] = time_emb[...].astype(F32)
    gains[...] = gain_sum.add()
    parts[0].fourth()
    parts[1].third()
    parts[2].third()
    first_norm(z, tok, time, gains, segs, xs, n1, bias)
    parts[0].fifth()
    parts[0].last()

    project(n1, W, pq, pv)
    parts[1].fourth()
    attention(0, 4, pq, pv, bias, probs, mx)
    parts[2].fourth()
    parts[1].fifth()
    attention(4, 8, pq, pv, bias, probs, mx)
    parts[2].fifth()
    second_norm(W, mx, xs, gains, mid, n2)
    parts[1].last()
    feed_out(1, 0, W, n2, act, slope, acc_out, True)
    feed_out(1, 1, W, n2, act, slope, acc_out, False)
    parts[2].last()
    feed_out(2, 0, W, n2, act, slope, acc_out, False)
    feed_out(2, 1, W, n2, act, slope, acc_out, False)
    tok[...] = (mid[...] + acc_out[...]).astype(BF)
    out_rows = Rows(net, tok, out, local_sem.at[9])
    out_rows.send()

    units = ((1, 0), (1, 1), (2, 0), (2, 1), (0, 0), (0, 1))
    sums = [
        Scatter(net, G, p, zp, 2 * max(p - 1, 0) + zp, cross, half, full, small) for p, zp in units
    ]
    deep = [Deep(net, G, p, tiny, done) for p in range(3)]

    def free():
        pl.semaphore_signal(free_sem, inc=1, device_id=place.device("c", 1), device_id_type=MESH)

    feed_back(1, 0, W, G, n2, ct, act, slope, acc_g, True)
    sums[0].to_core()
    feed_back(1, 1, W, G, n2, ct, act, slope, acc_g, False)
    sums[1].to_core()
    sums[0].add_core()
    free()
    feed_back(2, 0, W, G, n2, ct, act, slope, acc_g, False)
    sums[2].to_core()
    sums[1].add_core()
    free()
    sums[0].add_half()
    out_rows.forward(0)
    feed_back(2, 1, W, G, n2, ct, act, slope, acc_g, False)
    sums[3].to_core()
    sums[2].add_core()
    sums[1].add_half()
    second_back(mid, acc_g, ct, gains, br, ng)
    sums[3].add_core()
    sums[0].add_full()
    mixed_grad(W, br, slope)
    out_rows.forward(1)
    sums[2].add_half()
    attention_back(0, pq, pv, probs, slope, act, dpv)
    pl.semaphore_wait(free_sem, 2)
    first_grads(0, G, n1, br, mx, act, dpv)
    sums[4].to_core()
    sums[1].add_full()
    sums[3].add_half()
    attention_back(1, pq, pv, probs, slope, act, dpv)
    sums[4].add_core()
    sums[0].add_small()
    sums[2].add_full()
    input_grad_sum(W, act, dpv, acc_g)
    first_back(xs, acc_g, mid, gains, ng, n2)
    in_rows = Rows(net, n2, input_grad, local_sem.at[10])
    in_rows.send()
    norm_total = Sum(net, {"c": nc, "x": nx, "y": ny, "z": nz})
    norm_total.send("c", ng[...])
    first_grads(1, G, n1, br, mx, act, dpv)
    sums[5].to_core()
    sums[1].add_small()
    deep[1].send()
    sums[3].add_full()
    sums[4].add_half()
    sums[5].add_core()
    norm_total.send("x", norm_total.add())
    sums[2].add_small()
    sums[4].add_full()
    sums[5].add_half()
    norm_total.send("y", norm_total.add())
    sums[3].add_small()
    deep[2].send()
    in_rows.forward(0)
    sums[4].add_small()
    squares = deep[1].add()
    norm_total.send("z", norm_total.add())
    sums[5].add_full()
    sums[5].add_small()
    deep[0].send()
    in_rows.forward(1)
    squares = squares + deep[2].add()
    norm_rows = norm_total.add()
    norm_sum[...] = norm_rows
    squares = squares + deep[0].add()
    total = Sum(net, {"c": sc, "x": sx, "y": sy, "z": sz})
    total.send("c", jnp.full((8, 128), squares, F32))
    other_rows = pl.ds(pl.multiple_of(24 * (1 - core), 8), 24)
    own_rows = pl.ds(pl.multiple_of(24 * core, 8), 24)
    trade = net.group(shards.at[core])
    trade.push(done.at[:, other_rows, :], shards.at[core], "c", 1)
    shards[core] = done[:, own_rows, :]
    total.send("x", total.add())
    total.send("y", total.add())
    total.send("z", total.add())
    square_sum[...] = total.add() + jnp.sum(norm_rows * norm_rows)
    trade.arrive()
    out_rows.finish()
    in_rows.finish()
    net.finish()


def layer(tokens, time_emb, segs, cotangent, wq, wo, wu, wd, norm):
    V = pltpu.VMEM
    rows, low = (ROWS, D), BF
    anywhere = pl.BlockSpec(memory_space=pl.ANY)
    near = pl.BlockSpec(memory_space=pltpu.VMEM)
    return pl.pallas_call(
        layer_kernel,
        name="layer",
        out_shape=(
            jax.ShapeDtypeStruct(tokens.shape, BF),
            jax.ShapeDtypeStruct(tokens.shape, BF),
            jax.ShapeDtypeStruct((2, 3, 24, WIDE), F32),
            jax.ShapeDtypeStruct((8, D), F32),
            jax.ShapeDtypeStruct((8, 128), F32),
        ),
        in_specs=[anywhere] * 9,
        out_specs=[anywhere, anywhere, near, near, near],
        scratch_shapes=[
            V((3, 2, 2, 4, 4, 48, D), low),
            V((3, 2, 2, 4, 4, 48, D), low),
            V((4, 4, 4, 48, D), low),
            V((3, 2, 2, 2, 2, 48, WIDE), low),
            V((3, 2, 2, 2, 4, 48, WIDE), low),
            V((3, 2, 2, 3, 48, WIDE), low),
            V((3, 3, 48, WIDE), low),
            V((3, 48, WIDE), F32),
            V((2, 3, 24, WIDE), F32),
            V((3, 24, WIDE), F32),
            V((4, 8, D), F32),
            V((4, 8, D), F32),
            V((2, 8, D), F32),
            V((4, 8, D), F32),
            V((4, 8, D), F32),
            V((4, 8, D), F32),
            V((2, 8, D), F32),
            V((4, 8, 128), F32),
            V((4, 8, 128), F32),
            V((4, 8, 128), F32),
            V((2, 8, 128), F32),
            V((8, D), F32),
            V((16, D), F32),
            V((8, D), F32),
            V(rows, F32),
            V(rows, low),
            V((SEQS, LEN, LEN), F32),
            V((2, ROWS, D), low),
            V((4, ROWS, 256), low),
            V((SEQS, 4, WIDE, LEN), low),
            V((4, ROWS, 256), low),
            V(rows, F32),
            V(rows, low),
            V((4, ROWS, D), low),
            V((4, ROWS, D), low),
            V(rows, F32),
            V(rows, F32),
            V(rows, low),
            V((4, ROWS, 256), low),
            V(rows, low),
            V(rows, low),
            V(time_emb.shape, low),
            V(segs.shape, jnp.int32),
            V(wq.shape, F32),
            V(wo.shape, F32),
            V(wu.shape, F32),
            V(wd.shape, F32),
            V(norm.shape, F32),
            pltpu.SemaphoreType.DMA((GROUPS,)),
            pltpu.SemaphoreType.DMA((GROUPS,)),
            pltpu.SemaphoreType.DMA((11,)),
            pltpu.SemaphoreType.REGULAR,
        ],
        compiler_params=pltpu.CompilerParams(
            collective_id=0, has_side_effects=True, vmem_limit_bytes=64 * 2**20
        ),
    )(tokens, time_emb, segs, cotangent, wq, wo, wu, wd, norm)


def adam(weight, gradient, moment, second, step_rate, decay_rate):
    moment = BETA_ONE * moment + (1.0 - BETA_ONE) * gradient
    second = BETA_TWO * second + (1.0 - BETA_TWO) * gradient * gradient
    moment_hat = moment / (1.0 - BETA_ONE**STEP)
    second_hat = second / (1.0 - BETA_TWO**STEP)
    weight = weight - step_rate * (
        moment_hat / (jnp.sqrt(second_hat) + ADAM_EPS) + decay_rate * weight
    )
    return (moment, second, weight)


def step_kernel(
    out_in, grad_in, shards, norm_sum, square_sum, wq, wo, wu, wd, norm,
    qm, qs, om, os, um, us, dm, ds, nm, ns,
    out, grad, total, qm_new, qs_new, q_new, om_new, os_new, o_new, um_new, us_new, u_new, dm_new, ds_new, d_new,
    nm_new, ns_new, n_new, norm_grad, held, sem_in, sem_out,
):
    copies = []
    for k in range(8):
        rows = pl.ds(512 * (k % 4), 512)
        src, dst = ((out_in, out), (grad_in, grad))[k // 4]
        copies.append(
            (
                pltpu.make_async_copy(src.at[rows, :], held.at[k], sem_in.at[k]),
                pltpu.make_async_copy(held.at[k], dst.at[rows, :], sem_out.at[k]),
            )
        )
        copies[-1][0].start()
    grad_norm = jnp.sqrt(square_sum[0:1, 0:1])
    total[...] = grad_norm
    factor = jnp.minimum(1.0, CLIP_AT / (grad_norm + 1e-06))

    def put(refs, at, value):
        for ref, new in zip(refs, value):
            ref[at] = new

    first, second = shards[0, 0], shards[1, 0]
    tail = lambda v: jnp.concatenate([v[:, 256:], v[:, 192:256]], axis=1)
    for c, g in enumerate((first[:, :192], tail(first), second[:, :192])):
        put((qm_new, qs_new, q_new), c, adam(wq[c], g * factor, qm[c], qs[c], RATE_MATRIX, WEIGHT_DECAY))
    for came, copy in copies:
        came.wait()
        copy.start()
    put((om_new, os_new, o_new), ..., adam(wo[...], tail(second) * factor, om[...], os[...], RATE_OUT, WEIGHT_DECAY))
    for half in range(2):
        at = (slice(None), pl.ds(WIDE * half, WIDE))
        g = shards[0, 1 + half] * factor
        put((um_new, us_new, u_new), at, adam(wu[at], g, um[at], us[at], RATE_MATRIX, WEIGHT_DECAY))
        g = shards[1, 1 + half] * factor
        put((dm_new, ds_new, d_new), at, adam(wd[at], g, dm[at], ds[at], RATE_MATRIX, WEIGHT_DECAY))
    start = lax.axis_index("dp") * 24
    rolled = pltpu.roll(norm_sum[...], lax.rem(D - start, D), 1)
    g = rolled[0:4, 0:24] * factor
    norm_grad[...] = g
    put((nm_new, ns_new, n_new), ..., adam(norm[...], g, nm[...], ns[...], RATE_VECTOR, 0.0))
    for _, copy in copies:
        copy.wait()


def step(out_in, grad_in, shards, norm_sum, square_sum, weights, moments):
    anywhere = pl.BlockSpec(memory_space=pl.ANY)
    near = pl.BlockSpec(memory_space=pltpu.VMEM)
    like = lambda v: jax.ShapeDtypeStruct(v.shape, v.dtype)
    shapes = [like(out_in), like(grad_in), jax.ShapeDtypeStruct((1, 1), F32)]
    for w in weights:
        shapes += [like(w)] * 3
    shapes.append(like(weights[-1]))
    return pl.pallas_call(
        step_kernel,
        name="step",
        out_shape=shapes,
        in_specs=[anywhere] * 2 + [near] * (3 + len(weights) + len(moments)),
        out_specs=[anywhere] * 2 + [near] * (len(shapes) - 2),
        scratch_shapes=[
            pltpu.VMEM((8, ROWS, D), BF),
            pltpu.SemaphoreType.DMA((8,)),
            pltpu.SemaphoreType.DMA((8,)),
        ],
        compiler_params=pltpu.CompilerParams(vmem_limit_bytes=64 * 2**20),
    )(out_in, grad_in, shards, norm_sum, square_sum, *weights, *moments)


def body(
    tokens, time_emb, segments, cotangent, w_qkv, w_out, w_up, w_down, norm_params,
    qkv_first, qkv_second, out_first, out_second, up_first, up_second, down_first, down_second, norm_first, norm_second,
):
    weights = (w_qkv, w_out.T, w_up, w_down.T, norm_params)
    sent = layer(tokens, time_emb, segments, cotangent, *weights)
    moments = (
        qkv_first, qkv_second, out_first.T, out_second.T, up_first, up_second, down_first.T, down_second.T,
        norm_first, norm_second,
    )
    new = list(step(*sent, weights, moments))
    new[2] = new[2].reshape(())
    for k in (6, 7, 8, 12, 13, 14):
        new[k] = new[k].T
    return tuple(new)


def solution(mesh):
    return jax.shard_map(
        body,
        mesh=mesh,
        in_specs=(
            P("dp", None),
            P("dp", None),
            P("dp", None),
            P("dp", None),
            P(None, "dp", "mp"),
            P("mp", "dp"),
            P("dp", "mp"),
            P("mp", "dp"),
            P(None, "dp"),
            P(None, "dp", "mp"),
            P(None, "dp", "mp"),
            P("mp", "dp"),
            P("mp", "dp"),
            P("dp", "mp"),
            P("dp", "mp"),
            P("mp", "dp"),
            P("mp", "dp"),
            P(None, "dp"),
            P(None, "dp"),
        ),
        out_specs=(
            P("dp", None),
            P("dp", None),
            P(),
            P(None, "dp", "mp"),
            P(None, "dp", "mp"),
            P(None, "dp", "mp"),
            P("mp", "dp"),
            P("mp", "dp"),
            P("mp", "dp"),
            P("dp", "mp"),
            P("dp", "mp"),
            P("dp", "mp"),
            P("mp", "dp"),
            P("mp", "dp"),
            P("mp", "dp"),
            P(None, "dp"),
            P(None, "dp"),
            P(None, "dp"),
            P(None, "dp"),
        ),
        check_vma=False,
    )
```

```python
import jax
import jax.numpy as jnp
from jax import lax
from jax.experimental import pallas as pl
from jax.experimental.pallas import tpu as pltpu
from jax.sharding import PartitionSpec as P

MESH = pl.DeviceIdType.MESH

BF = jnp.bfloat16
F32 = jnp.float32
HEAD = 64
LEN = 128
ROWS = 512
D = 768
SEQS = 4
WIDE = 384
CLIP_AT = 1.0
BETA_ONE = 0.9
BETA_TWO = 0.95
ADAM_EPS = 1e-08
STEP = 10
WEIGHT_DECAY = 0.01
RATE_MATRIX = 0.05
RATE_OUT = 0.3
RATE_VECTOR = 0.5
GROUPS = 64
NORM_EPS = 1e-05


def nn(a, b):
    return jnp.dot(a, b, preferred_element_type=F32)


def nt(a, b):
    return lax.dot_general(a, b, (((1,), (1,)), ((), ())), preferred_element_type=F32)


def tn(a, b):
    return lax.dot_general(a, b, (((0,), (0,)), ((), ())), preferred_element_type=F32)


def whole(W, p, owner, zp):
    return W[p, owner, zp].reshape(D, D)


def columns(W, zp, base):
    return W[0, 1, zp, :, :, :, base : base + 256].reshape(D, 256)


def tiles(x):
    return x.astype(BF).reshape(4, 4, 48, x.shape[1])


def norm_stats(x):
    center = jnp.mean(x, axis=-1, keepdims=True)
    off = x - center
    inv = lax.rsqrt(jnp.mean(off * off, axis=-1, keepdims=True) + NORM_EPS)
    return off * inv, inv


def low_lanes(x):
    lane = lax.broadcasted_iota(jnp.int32, x.shape, x.ndim - 1)
    return lane < HEAD


def split_heads(x):
    first = low_lanes(x)
    zero = jnp.zeros_like(x)
    return jnp.concatenate([jnp.where(first, x, zero), jnp.where(first, zero, x)], axis=0)


def swap_halves(x):
    return pltpu.roll(x.astype(F32), HEAD, 1).astype(x.dtype)


def seq_rows(s):
    return pl.ds(pl.multiple_of(s * LEN, LEN), LEN)


def first_norm(place, tok, time, gains, segs, xs, n1, bias):
    for s in range(SEQS):
        rows = slice(s * LEN, s * LEN + LEN)
        x = tok[rows, :].astype(F32) + time[pl.ds(SEQS * place + s, 1), :]
        xs[rows, :] = x
        scaled, _ = norm_stats(x)
        n1[rows, :] = (scaled * gains[0:1, :] + gains[1:2, :]).astype(BF)
        lab = jnp.broadcast_to(segs[pl.ds(SEQS * place + s, 1), :].astype(F32), (LEN, LEN))
        bias[s] = jnp.where(lab == lab.T, 0.0, -1e30).astype(F32)


def project(h, n1, W, pq, pv):
    rows = slice(256 * h, 256 * h + 256)
    for zp in range(2):
        pq[zp, rows, :] = nn(n1[rows, :], whole(W, 0, 0, zp)).astype(BF)
        for j in range(2):
            pv[2 * zp + j, rows, :] = nn(n1[rows, :], columns(W, zp, 384 * j)).astype(BF)


def softmax_columns(scores):
    e = jnp.exp(scores - jnp.max(scores, axis=1, keepdims=True))
    return (e * (1.0 / jnp.sum(e, axis=1, keepdims=True))).astype(BF)


def value_two(vg):
    first = low_lanes(vg)
    return swap_halves(jnp.where(first, vg, jnp.zeros_like(vg)))


def attention(lo, hi, pq, pv, bias, probs, mx):
    scaling = HEAD ** (-0.5)

    def step(i, _):
        s, zp = i // 2, i % 2
        rows = seq_rows(s)
        mask = bias[s]
        for j in range(2):
            z = 2 * zp + j
            base = 384 * j
            ga = pq[zp, rows, base : base + 128]
            gb = pq[zp, rows, base + 128 : base + 256]
            gc = pq[zp, rows, base + 256 : base + 384]
            va = pv[z, rows, 0:128]
            vb = value_two(pv[z, rows, 128:256])
            both = swap_halves(gb)
            first = low_lanes(gb)
            s01 = nt(split_heads(gc), ga)
            s2 = nt(jnp.where(first, both, jnp.zeros_like(gb)), gb)
            scores = jnp.concatenate([s01, s2], axis=0).reshape(3, LEN, LEN)
            p = softmax_columns(scores * scaling + mask[None]).reshape(3 * LEN, LEN)
            probs[s, z] = p
            mx[z, rows, 128:256] = tn(p[: 2 * LEN], split_heads(va)).astype(BF)
            mx[z, rows, 0:128] = tn(p[2 * LEN :], vb).astype(BF)
        return 0

    lax.fori_loop(lo, hi, step, 0, unroll=4)


def second_norm(h, W, mx, xs, gains, mid, n2):
    rows = slice(256 * h, 256 * h + 256)
    acc = xs[rows, :]
    for z in range(4):
        base = 384 * (z % 2) + 128
        acc = acc + nt(mx[z, rows, :], columns(W, z // 2, base))
    mid[rows, :] = acc
    scaled, _ = norm_stats(acc)
    n2[rows, :] = (scaled * gains[2:3, :] + gains[3:4, :]).astype(BF)


def gelu_parts(u):
    cdf = 0.5 * (1.0 + lax.erf(u * 0.7071067811865476))
    pdf = jnp.exp(u * u * -0.5) * 0.3989422804014327
    return u * cdf, cdf + u * pdf


def feed_out(h, p, zp, W, n2, act, slope, acc_out):
    at = 2 * (p - 1) + zp
    rows = slice(256 * h, 256 * h + 256)
    a, rate = gelu_parts(nn(n2[rows, :], whole(W, p, 0, zp)))
    a = a.astype(BF)
    act[at, rows, :] = a
    slope[at, rows, :] = rate.astype(BF)
    out = nt(a, whole(W, p, 1, zp))
    if at == 0:
        acc_out[rows, :] = out
    else:
        acc_out[rows, :] += out


def layer_rows(h, mid, acc_out, rows_out):
    rows = slice(256 * h, 256 * h + 256)
    rows_out[rows, :] = (mid[rows, :] + acc_out[rows, :]).astype(BF)


def feed_back(p, zp, W, ct, slope, acc_g):
    at = 2 * (p - 1) + zp
    for h in range(2):
        rows = slice(256 * h, 256 * h + 256)
        slope[at, rows, :] = (nn(ct[rows, :], whole(W, p, 1, zp)) * slope[at, rows, :].astype(F32)).astype(BF)
    back = nt(slope[at], whole(W, p, 0, zp))
    if at == 0:
        acc_g[...] = back
    else:
        acc_g[...] += back


def feed_grads(p, zp, G, n2, ct, act, slope):
    at = 2 * (p - 1) + zp
    G[p, 1, zp] = tiles(tn(ct[...], act[at]))
    G[p, 0, zp] = tiles(tn(n2[...], slope[at]))


def norm_back(grad, scaled, inv, gain):
    u = grad * gain
    m1 = jnp.mean(u, axis=-1, keepdims=True)
    m2 = jnp.mean(u * scaled, axis=-1, keepdims=True)
    return inv * (u - m1 - scaled * m2)


def second_back(mid, acc_g, ct, gains, br, ng):
    ng[4:8, :] = jnp.zeros((4, D), F32)
    scaled, inv = norm_stats(mid[...])
    g = acc_g[...]
    ng[2:3, :] = jnp.sum(g * scaled, axis=0, keepdims=True)
    ng[3:4, :] = jnp.sum(g, axis=0, keepdims=True)
    gm = ct[...].astype(F32) + norm_back(g, scaled, inv, gains[2:3, :])
    mid[...] = gm
    br[...] = gm.astype(BF)


def mixed_grad(W, br, dm):
    for z in range(4):
        base = 384 * (z % 2) + 128
        dm[z // 2, :, base - 128 : base + 128] = nn(br[...], columns(W, z // 2, base)).astype(BF)


def attention_back(lo, hi, zp, pq, pv, probs, dm, dpq, dpv):
    scaling = HEAD ** (-0.5)

    def step(s, _):
        rows = seq_rows(s)
        for j in range(2):
            z = 2 * zp + j
            base = 384 * j
            ga = pq[zp, rows, base : base + 128]
            gb = pq[zp, rows, base + 128 : base + 256]
            gc = pq[zp, rows, base + 256 : base + 384]
            va = pv[z, rows, 0:128]
            vb = value_two(pv[z, rows, 128:256])
            p = probs[s, z]
            db = dm[zp, rows, base : base + 128]
            da = dm[zp, rows, base + 128 : base + 256]
            gp = jnp.concatenate([nt(split_heads(va), da), nt(vb, db)], axis=0).reshape(3, LEN, LEN)
            pf = p.astype(F32).reshape(3, LEN, LEN)
            ds = (pf * (gp - jnp.sum(gp * pf, axis=1, keepdims=True))).astype(BF).reshape(3 * LEN, LEN)
            beside = lambda v: jnp.concatenate([v[:LEN], v[LEN : 2 * LEN]], axis=1)
            dv01 = nn(beside(p), split_heads(da))
            dk01 = nn(beside(ds), split_heads(ga)) * scaling
            dq01 = tn(ds[: 2 * LEN], split_heads(gc)) * scaling
            dv2 = pltpu.roll(nn(p[2 * LEN :], db), HEAD, 1)
            both = swap_halves(gb)
            dk2 = nn(ds[2 * LEN :], both)
            dq2 = tn(ds[2 * LEN :], both)
            first = low_lanes(dq2)
            dpq[zp, rows, base : base + 128] = dq01.astype(BF)
            dpq[zp, rows, base + 128 : base + 256] = (jnp.where(first, dq2, dk2) * scaling).astype(BF)
            dpq[zp, rows, base + 256 : base + 384] = dk01.astype(BF)
            dpv[2 + zp, rows, base : base + 128] = dv01.astype(BF)
            dpv[2 + zp, rows, base + 128 : base + 256] = jnp.where(first, dv2, 0.0).astype(BF)
        return 0

    lax.fori_loop(lo, hi, step, 0, unroll=2)


def input_grad_sum(W, dpq, dpv, gn):
    acc = nt(dpq[0], whole(W, 0, 0, 0)) + nt(dpq[1], whole(W, 0, 0, 1))
    for z in range(4):
        acc = acc + nt(dpv[2 + z // 2, :, 384 * (z % 2) : 384 * (z % 2) + 256], columns(W, z // 2, 384 * (z % 2)))
    gn[...] = acc


def first_grads(zp, G, n1, br, mx, dpq, dpv):
    G[0, 0, zp] = tiles(tn(n1[...], dpq[zp]))
    for j in range(2):
        z = 2 * zp + j
        base = 384 * j
        gv = tn(n1[...], dpv[2 + zp, :, base : base + 256])
        go = tn(br[...], mx[z])
        G[0, 1, zp, :, :, :, base : base + 128] = tiles(gv[:, :128])
        G[0, 1, zp, :, :, :, base + 128 : base + 256] = tiles(gv[:, 128:] + go[:, :128])
        G[0, 1, zp, :, :, :, base + 256 : base + 384] = tiles(go[:, 128:])


def first_back(h, xs, gn, mid, gains, ng, dx):
    rows = slice(256 * h, 256 * h + 256)
    scaled, inv = norm_stats(xs[rows, :])
    g = gn[rows, :]
    gain = jnp.sum(g * scaled, axis=0, keepdims=True)
    shift = jnp.sum(g, axis=0, keepdims=True)
    if h == 0:
        ng[0:1, :] = gain
        ng[1:2, :] = shift
    else:
        ng[0:1, :] += gain
        ng[1:2, :] += shift
    dx[rows, :] = (mid[rows, :] + norm_back(g, scaled, inv, gains[0:1, :])).astype(BF)


class Place:
    def __init__(self):
        dp = lax.axis_index("dp")
        self.dp = dp
        self.at = {"z": lax.axis_index("mp"), "y": dp // 8, "x": (dp // 2) % 4, "c": dp % 2}

    def step(self, axis, d):
        return (self.at[axis] + d) % (2 if axis == "c" else 4)

    def device(self, **moves):
        q = {axis: self.step(axis, moves.get(axis, 0)) for axis in self.at}
        return ((q["y"] * 4 + q["x"]) * 2 + q["c"], q["z"])


NEAR = [{axis: d} for axis in ("x", "y", "z") for d in (1, 2, 3)] + [{"c": 1}]


class Net:
    def __init__(self, place, send_sem, recv_sem):
        self.place, self.send_sem, self.recv_sem = place, send_sem, recv_sem
        self.groups = []

    def group(self, like):
        group = Group(self, len(self.groups), like)
        self.groups.append(group)
        return group

    def finish(self):
        for group in self.groups:
            group.every.wait_send()


class Group:
    def __init__(self, net, k, like):
        self.net, self.k = net, k
        self.every = self.copy(like, like, net.place.device(c=1))

    def copy(self, src, dst, to):
        return pltpu.make_async_remote_copy(
            src_ref=src,
            dst_ref=dst,
            send_sem=self.net.send_sem.at[self.k],
            recv_sem=self.net.recv_sem.at[self.k],
            device_id=to,
            device_id_type=MESH,
        )

    def push(self, src, dst, axis, d):
        self.copy(src, dst, self.net.place.device(**{axis: d})).start()

    def arrive(self):
        self.every.wait_recv()


def lanes(z):
    return pl.ds(pl.multiple_of((z % 2) * WIDE, 128), WIDE)


def weight_view(W, p, owner, r, at):
    y = slice(None) if at["y"] is None else at["y"]
    x = slice(None) if at["x"] is None else at["x"]
    rows = pl.ds(16 * r, 16)
    if at["z"] is None:
        return W.at[p, owner, :, y, x, rows, :]
    return W.at[p, owner, at["z"] // 2, y, x, rows, lanes(at["z"])]


ORDERS = (("x", "y", "z"), ("y", "z", "x"), ("z", "x", "y"))


class Gather:
    def __init__(self, net, W, p):
        self.net, self.W, self.p = net, W, p
        self.core = net.place.at["c"]
        self.across = net.group(W.at[p, self.core])

    def view(self, r, at):
        return weight_view(self.W, self.p, self.core, r, at)

    def known(self, r, done, **moved):
        at = dict(self.net.place.at)
        for axis in ORDERS[r][:done]:
            at[axis] = None
        at.update(moved)
        return at

    def spread(self, done, ds, like):
        self.step = self.net.group(like)
        for r in range(3):
            src = self.view(r, self.known(r, done))
            for d in ds:
                self.step.push(src, src, ORDERS[r][done], d)

    def share(self, r, at):
        src = self.view(r, at)
        self.across.push(src, src, "c", 1)

    def first(self):
        self.spread(0, (1, 3, 2), self.W.at[self.p, self.core, 0, 0, 0:3, :, 0:WIDE])

    def second(self):
        self.step.arrive()
        self.spread(1, (1, 3, 2), self.W.at[self.p, self.core, 0, :, 0:3, :, 0:WIDE])

    def third(self):
        self.step.arrive()
        self.spread(2, (1, 3), self.W.at[self.p, self.core, 0])
        for r in range(3):
            self.share(r, self.known(r, 2))

    def fourth(self):
        self.step.arrive()
        self.step = self.net.group(self.W.at[self.p, self.core, 0, :, :, :, 0:WIDE])
        for r in range(3):
            axis = ORDERS[r][2]
            cut = "x" if axis == "y" else "y"
            for side, d in ((0, 1), (1, 3)):
                half = {axis: self.net.place.step(axis, -d), cut: pl.ds(2 * side, 2)}
                src = self.view(r, self.known(r, 2, **half))
                self.step.push(src, src, axis, d)
        for r in range(3):
            axis = ORDERS[r][2]
            for d in (3, 1):
                self.share(r, self.known(r, 2, **{axis: self.net.place.step(axis, d)}))

    def fifth(self):
        self.step.arrive()
        for r in range(3):
            axis = ORDERS[r][2]
            self.share(r, self.known(r, 2, **{axis: self.net.place.step(axis, 2)}))

    def last(self):
        self.across.arrive()


class Scatter:
    def __init__(self, net, G, p, zp, slot, cross, half, full, small):
        self.net, self.G, self.p, self.zp, self.slot = net, G, p, zp, slot
        self.cross, self.half, self.full, self.small = cross, half, full, small
        self.core = net.place.at["c"]

    def view(self, j, y, x):
        return (self.p, self.core, self.zp, y, x, slice(None), pl.ds(WIDE * j, WIDE))

    def block(self, j, d, cut=slice(None)):
        if j == 0:
            return self.view(0, cut, self.net.place.step("x", d))
        return self.view(1, self.net.place.step("y", d), cut)

    def own(self, j, d):
        at = self.net.place.at
        if j == 0:
            return self.view(0, self.net.place.step("y", d), at["x"])
        return self.view(1, at["y"], self.net.place.step("x", d))

    def to_core(self):
        dst = self.cross.at[self.slot]
        self.step = self.net.group(dst)
        self.step.push(self.G.at[self.p, 1 - self.core, self.zp], dst, "c", 1)

    def add_core(self):
        self.step.arrive()

        def per_y(y, _):
            at = (self.p, self.core, self.zp, y)
            self.G[at] = self.G[at] + self.cross[self.slot, y]
            return 0

        lax.fori_loop(0, 4, per_y, 0)
        self.step = self.net.group(self.half.at[self.slot])
        for side, d in ((0, 1), (1, 3)):
            for j, axis in ((0, "x"), (1, "y")):
                src = self.G.at[self.block(j, 2, pl.ds(2 * side, 2))]
                self.step.push(src, self.half.at[self.slot, j, side], axis, d)

    def add_half(self):
        self.step.arrive()
        self.step = self.net.group(self.full.at[self.p, self.zp])
        for side, d in ((0, 1), (1, 3)):
            for j, axis in ((0, "x"), (1, "y")):
                at = self.block(j, d, pl.ds(2 * side, 2))
                self.G[at] = self.G[at] + self.half[self.slot, j, side]
                self.step.push(self.G.at[self.block(j, d)], self.full.at[self.p, self.zp, j, side], axis, d)

    def add_full(self):
        self.step.arrive()
        self.step = self.net.group(self.small.at[self.p, self.zp])
        for j, axis in ((0, "y"), (1, "x")):
            at = self.block(j, 0)
            total = self.G[at].astype(F32)
            for side in range(2):
                total = total + self.full[self.p, self.zp, j, side].astype(F32)
            self.G[at] = total.astype(BF)
            for d in (1, 3, 2):
                self.step.push(self.G.at[self.own(j, d)], self.small.at[self.p, self.zp, j, d - 1], axis, d)

    def add_small(self):
        self.step.arrive()
        for j in range(2):
            at = self.own(j, 0)
            total = self.G[at].astype(F32)
            for d in range(3):
                total = total + self.small[self.p, self.zp, j, d].astype(F32)
            self.G[at] = total.astype(BF)


class Deep:
    def __init__(self, net, G, p, tiny, done):
        self.net, self.G, self.p, self.tiny, self.done = net, G, p, tiny, done

    def chunk(self, d):
        at = self.net.place.at
        z = self.net.place.step("z", d)
        return (self.p, at["c"], z // 2, at["y"], at["x"], slice(None), lanes(z))

    def send(self):
        self.step = self.net.group(self.tiny.at[self.p])
        for d in (1, 3, 2):
            self.step.push(self.G.at[self.chunk(d)], self.tiny.at[self.p, d - 1], "z", d)

    def add(self):
        self.step.arrive()
        total = self.G[self.chunk(0)].astype(F32)
        for d in range(3):
            total = total + self.tiny[self.p, d].astype(F32)
        self.done[self.p] = total
        return jnp.sum(total * total)


class Sum:
    def __init__(self, net, slots):
        self.net, self.slots = net, slots

    def send(self, axis, value):
        slots = self.slots[axis]
        here = self.net.place.at[axis]
        self.axis = axis
        slots[here] = value
        ds = (1,) if axis == "c" else (1, 3, 2)
        self.step = self.net.group(slots.at[0 : len(ds)])
        for d in ds:
            self.step.push(slots.at[here], slots.at[here], axis, d)

    def add(self):
        self.step.arrive()
        slots = self.slots[self.axis]
        total = slots[0]
        for k in range(1, slots.shape[0]):
            total = total + slots[k]
        return total


class Rows:
    def __init__(self, net, rows_ref, out, sem):
        self.net, self.rows_ref, self.out, self.sem = net, rows_ref, out, sem
        self.near, self.local = [], []
        self.far = net.group(out.at[0:ROWS, :])

    def place_of(self, d, piece, side=None):
        start = ROWS * self.net.place.step("z", d) + 256 * piece
        if side is None:
            return self.out.at[pl.ds(pl.multiple_of(start, 256), 256), :]
        return self.out.at[pl.ds(pl.multiple_of(start + 128 * side, 128), 128), :]

    def send(self, piece):
        src = self.rows_ref.at[pl.ds(256 * piece, 256), :]
        near = self.net.group(self.out.at[0:ROWS, :])
        self.near.append(near)
        for d in (1, 3):
            near.push(src, self.place_of(0, piece), "z", d)
        self.local.append(pltpu.make_async_copy(src, self.place_of(0, piece), self.sem.at[piece]))
        self.local[piece].start()

    def forward(self, piece):
        self.near[piece].arrive()
        for side, d in ((0, 1), (1, 3)):
            src = self.place_of(-d, piece, side)
            self.far.push(src, src, "z", d)

    def finish(self):
        self.far.arrive()
        for copy in self.local:
            copy.wait()


def pack(wq, wo, wu, wd, keep):
    q, k, v, o = wq[0], wq[1], wq[2], wo[...]
    keep[0, 0] = jnp.concatenate([q, k[:, 128:], k[:, :128]], axis=1)
    keep[1, 0] = jnp.concatenate([v, o[:, 128:], o[:, :128]], axis=1)
    for half in range(2):
        keep[0, 1 + half] = wu[:, WIDE * half : WIDE * half + WIDE]
        keep[1, 1 + half] = wd[:, WIDE * half : WIDE * half + WIDE]


def layer_kernel(
    tokens, time_in, segs_in, cotangent, wq_in, wo_in, wu_in, wd_in, norm_in,
    out, input_grad, shards, norm_sum, square_sum,
    W, G, cross, half, full, small, tiny, done, keep, other,
    gx, gy, gc, nx, ny, nz, nc, sx, sy, sz, sc, gains, time, ng,
    xs, n1, bias, pq, pv, probs, mx, mid, n2, act, slope, acc_out, acc_g, tok, ct,
    time_emb, segs, wq, wo, wu, wd, norm,
    send_sem, recv_sem, local_sem, out_sem, in_sem, free_sem,
):
    place = Place()
    net = Net(place, send_sem, recv_sem)
    z, core = place.at["z"], place.at["c"]
    mine = pl.ds(pl.multiple_of(ROWS * z, ROWS), ROWS)
    pairs = (
        (wq_in, wq), (wo_in, wo), (wu_in, wu), (wd_in, wd), (norm_in, norm),
        (time_in, time_emb), (segs_in, segs), (tokens.at[mine, :], tok), (cotangent.at[mine, :], ct),
    )
    loads = [pltpu.make_async_copy(src, dst, local_sem.at[i]) for i, (src, dst) in enumerate(pairs)]
    for load in loads:
        load.start()
    barrier = pltpu.get_barrier_semaphore()
    for moves in NEAR:
        pl.semaphore_signal(barrier, inc=1, device_id=place.device(**moves), device_id_type=MESH)
    for load in loads[:5]:
        load.wait()
    pack(wq, wo, wu, wd, keep)
    column = lax.broadcasted_iota(jnp.int32, (24, D), 1)
    row = lax.broadcasted_iota(jnp.int32, (24, D), 0)
    spot = jnp.where(column == row + 24 * place.dp, 1.0, 0.0).astype(F32)
    rounded = norm[...].astype(BF).astype(F32)
    spread = jnp.concatenate([nn(rounded, spot), jnp.zeros((4, D), F32)], axis=0)
    pl.semaphore_wait(barrier, len(NEAR))

    swap = net.group(other)
    swap.push(keep.at[1 - core], other, "c", 1)
    gain_sum = Sum(net, {"x": gx, "y": gy, "c": gc})
    gain_sum.send("x", spread)
    swap.arrive()
    for p in range(3):
        kept = keep[core, p]
        came = other[p]
        even = core == 0
        rows = jnp.concatenate([jnp.where(even, kept, came), jnp.where(even, came, kept)], axis=0)
        W[p, core, z // 2, place.at["y"], place.at["x"], :, lanes(z)] = rows.astype(BF)
    parts = [Gather(net, W, p) for p in range(3)]
    for part in parts:
        part.first()
    gain_sum.send("y", gain_sum.add())
    parts[0].second()
    parts[1].second()
    gain_sum.send("c", gain_sum.add())
    parts[0].third()
    parts[2].second()
    for load in loads[5:]:
        load.wait()
    time[...] = time_emb[...].astype(F32)
    gains[...] = gain_sum.add()
    parts[0].fourth()
    parts[1].third()
    parts[2].third()
    first_norm(z, tok, time, gains, segs, xs, n1, bias)
    parts[0].fifth()
    parts[0].last()

    out_rows = Rows(net, tok, out, out_sem)
    in_rows = Rows(net, pq.at[0], input_grad, in_sem)
    norm_total = Sum(net, {"c": nc, "x": nx, "y": ny, "z": nz})
    units = ((1, 0), (1, 1), (2, 0), (2, 1), (0, 0), (0, 1))
    sums = [Scatter(net, G, p, zp, 2 * max(p - 1, 0) + zp, cross, half, full, small) for p, zp in units]
    deep = [Deep(net, G, p, tiny, done) for p in range(3)]
    squares = [None] * 3

    def free():
        pl.semaphore_signal(free_sem, inc=1, device_id=place.device(c=1), device_id_type=MESH)

    project(0, n1, W, pq, pv)
    parts[1].fourth()
    attention(0, 4, pq, pv, bias, probs, mx)
    parts[2].fourth()
    second_norm(0, W, mx, xs, gains, mid, n2)
    project(1, n1, W, pq, pv)
    parts[1].fifth()
    attention(4, 8, pq, pv, bias, probs, mx)
    parts[2].fifth()
    second_norm(1, W, mx, xs, gains, mid, n2)
    parts[1].last()
    feed_out(0, 1, 0, W, n2, act, slope, acc_out)
    feed_out(1, 1, 0, W, n2, act, slope, acc_out)
    feed_back(1, 0, W, ct, slope, acc_g)
    feed_grads(1, 0, G, n2, ct, act, slope)
    sums[0].to_core()
    feed_out(0, 1, 1, W, n2, act, slope, acc_out)
    parts[2].last()
    feed_out(0, 2, 0, W, n2, act, slope, acc_out)
    feed_out(0, 2, 1, W, n2, act, slope, acc_out)
    layer_rows(0, mid, acc_out, tok)
    out_rows.send(0)
    feed_out(1, 1, 1, W, n2, act, slope, acc_out)
    sums[0].add_core()
    free()
    feed_back(1, 1, W, ct, slope, acc_g)
    feed_grads(1, 1, G, n2, ct, act, slope)
    sums[1].to_core()
    feed_out(1, 2, 0, W, n2, act, slope, acc_out)
    feed_out(1, 2, 1, W, n2, act, slope, acc_out)
    sums[0].add_half()
    layer_rows(1, mid, acc_out, tok)
    out_rows.send(1)
    feed_back(2, 0, W, ct, slope, acc_g)
    sums[1].add_core()
    free()
    feed_grads(2, 0, G, n2, ct, act, slope)
    sums[2].to_core()
    feed_back(2, 1, W, ct, slope, acc_g)
    feed_grads(2, 1, G, n2, ct, act, slope)
    sums[3].to_core()
    out_rows.forward(0)
    sums[0].add_full()
    second_back(mid, acc_g, ct, gains, n2, ng)
    sums[2].add_core()
    sums[1].add_half()
    mixed_grad(W, n2, slope)
    attention_back(0, 2, 0, pq, pv, probs, slope, act, slope)
    sums[3].add_core()
    attention_back(2, 4, 0, pq, pv, probs, slope, act, slope)
    sums[0].add_small()
    first_grads(0, G, n1, n2, mx, act, slope)
    pl.semaphore_wait(free_sem, 1)
    sums[4].to_core()
    sums[2].add_half()
    out_rows.forward(1)
    attention_back(0, 2, 1, pq, pv, probs, slope, act, slope)
    attention_back(2, 4, 1, pq, pv, probs, slope, act, slope)
    sums[1].add_full()
    sums[4].add_core()
    sums[3].add_half()
    first_grads(1, G, n1, n2, mx, act, slope)
    pl.semaphore_wait(free_sem, 1)
    sums[5].to_core()
    input_grad_sum(W, act, slope, acc_g)
    first_back(0, xs, acc_g, mid, gains, ng, pq.at[0])
    in_rows.send(0)
    sums[2].add_full()
    first_back(1, xs, acc_g, mid, gains, ng, pq.at[0])
    in_rows.send(1)
    norm_total.send("c", ng[...])
    sums[1].add_small()
    deep[1].send()
    sums[5].add_core()
    sums[4].add_half()
    norm_total.send("x", norm_total.add())
    sums[3].add_full()
    sums[2].add_small()
    sums[5].add_half()
    sums[4].add_full()
    norm_total.send("y", norm_total.add())
    in_rows.forward(0)
    sums[3].add_small()
    deep[2].send()
    sums[5].add_full()
    norm_total.send("z", norm_total.add())
    sums[4].add_small()
    squares[1] = deep[1].add()
    sums[5].add_small()
    deep[0].send()
    in_rows.forward(1)
    squares[2] = deep[2].add()
    norm_rows = norm_total.add()
    squares[0] = deep[0].add()
    norm_sum[...] = norm_rows
    other_rows = pl.ds(pl.multiple_of(24 * (1 - core), 8), 24)
    own_rows = pl.ds(pl.multiple_of(24 * core, 8), 24)
    trade = net.group(shards.at[core])
    trade.push(done.at[:, other_rows, :], shards.at[core], "c", 1)
    total = Sum(net, {"c": sc, "x": sx, "y": sy, "z": sz})
    total.send("c", jnp.full((8, 128), squares[0] + squares[1] + squares[2], F32))
    shards[core] = done[:, own_rows, :]
    total.send("x", total.add())
    total.send("y", total.add())
    total.send("z", total.add())
    square_sum[...] = total.add() + jnp.sum(norm_rows * norm_rows)
    trade.arrive()
    out_rows.finish()
    in_rows.finish()
    net.finish()


def layer(tokens, time_emb, segs, cotangent, wq, wo, wu, wd, norm):
    V = pltpu.VMEM
    rows, low = (ROWS, D), BF
    anywhere = pl.BlockSpec(memory_space=pl.ANY)
    near = pl.BlockSpec(memory_space=pltpu.VMEM)
    return pl.pallas_call(
        layer_kernel,
        name="layer",
        out_shape=(
            jax.ShapeDtypeStruct(tokens.shape, BF),
            jax.ShapeDtypeStruct(tokens.shape, BF),
            jax.ShapeDtypeStruct((2, 3, 24, WIDE), F32),
            jax.ShapeDtypeStruct((8, D), F32),
            jax.ShapeDtypeStruct((8, 128), F32),
        ),
        in_specs=[anywhere] * 9,
        out_specs=[anywhere, anywhere, near, near, near],
        scratch_shapes=[
            V((3, 2, 2, 4, 4, 48, D), low),
            V((3, 2, 2, 4, 4, 48, D), low),
            V((4, 4, 4, 48, D), low),
            V((4, 2, 2, 2, 48, WIDE), low),
            V((3, 2, 2, 2, 4, 48, WIDE), low),
            V((3, 2, 2, 3, 48, WIDE), low),
            V((3, 3, 48, WIDE), low),
            V((3, 48, WIDE), F32),
            V((2, 3, 24, WIDE), F32),
            V((3, 24, WIDE), F32),
            V((4, 8, D), F32),
            V((4, 8, D), F32),
            V((2, 8, D), F32),
            V((4, 8, D), F32),
            V((4, 8, D), F32),
            V((4, 8, D), F32),
            V((2, 8, D), F32),
            V((4, 8, 128), F32),
            V((4, 8, 128), F32),
            V((4, 8, 128), F32),
            V((2, 8, 128), F32),
            V((8, D), F32),
            V((16, D), F32),
            V((8, D), F32),
            V(rows, F32),
            V(rows, low),
            V((SEQS, LEN, LEN), F32),
            V((2, ROWS, D), low),
            V((4, ROWS, 256), low),
            V((SEQS, 4, WIDE, LEN), low),
            V((4, ROWS, 256), low),
            V(rows, F32),
            V(rows, low),
            V((4, ROWS, D), low),
            V((4, ROWS, D), low),
            V(rows, F32),
            V(rows, F32),
            V(rows, low),
            V(rows, low),
            V(time_emb.shape, low),
            V(segs.shape, jnp.int32),
            V(wq.shape, F32),
            V(wo.shape, F32),
            V(wu.shape, F32),
            V(wd.shape, F32),
            V(norm.shape, F32),
            pltpu.SemaphoreType.DMA((GROUPS,)),
            pltpu.SemaphoreType.DMA((GROUPS,)),
            pltpu.SemaphoreType.DMA((9,)),
            pltpu.SemaphoreType.DMA((2,)),
            pltpu.SemaphoreType.DMA((2,)),
            pltpu.SemaphoreType.REGULAR,
        ],
        compiler_params=pltpu.CompilerParams(
            collective_id=0, has_side_effects=True, vmem_limit_bytes=64 * 2**20
        ),
    )(tokens, time_emb, segs, cotangent, wq, wo, wu, wd, norm)


def adam(weight, gradient, moment, second, step_rate, decay_rate):
    moment = BETA_ONE * moment + (1.0 - BETA_ONE) * gradient
    second = BETA_TWO * second + (1.0 - BETA_TWO) * gradient * gradient
    moment_hat = moment / (1.0 - BETA_ONE**STEP)
    second_hat = second / (1.0 - BETA_TWO**STEP)
    weight = weight - step_rate * (
        moment_hat / (jnp.sqrt(second_hat) + ADAM_EPS) + decay_rate * weight
    )
    return (moment, second, weight)


def step_kernel(*refs):
    out_in, grad_in, *ins = refs[:20]
    out, grad, *outs = refs[20:39]
    held, kept, made, row_in, row_out, sem_in, sem_out = refs[39], refs[40:58], refs[58:75], *refs[75:]
    loads = [pltpu.make_async_copy(src, dst, sem_in.at[k]) for k, (src, dst) in enumerate(zip(ins, kept))]
    rows = []
    for k in range(8):
        at = pl.ds(ROWS * (k % 4), ROWS)
        src, dst = ((out_in, out), (grad_in, grad))[k // 4]
        rows.append(
            (
                pltpu.make_async_copy(src.at[at, :], held.at[k], row_in.at[k]),
                pltpu.make_async_copy(held.at[k], dst.at[at, :], row_out.at[k]),
            )
        )
    for load in loads:
        load.start()
    for came, _ in rows:
        came.start()
    for load in loads:
        load.wait()
    for came, leave in rows[:4]:
        came.wait()
        leave.start()
    shards, norm_sum, square_sum, wq, wo, wu, wd, norm, qm, qs, om, os, um, us, dm, ds, nm, ns = kept
    total, qm_new, qs_new, q_new, om_new, os_new, o_new, um_new, us_new, u_new = made[:10]
    dm_new, ds_new, d_new, nm_new, ns_new, n_new, norm_grad = made[10:]
    grad_norm = jnp.sqrt(square_sum[0:1, 0:1])
    total[...] = grad_norm
    factor = jnp.minimum(1.0, CLIP_AT / (grad_norm + 1e-06))

    def put(refs, at, value):
        for ref, new in zip(refs, value):
            ref[at] = new

    first, second = shards[0, 0], shards[1, 0]
    tail = lambda v: jnp.concatenate([v[:, 256:], v[:, 192:256]], axis=1)
    for c, g in enumerate((first[:, :192], tail(first), second[:, :192])):
        put((qm_new, qs_new, q_new), c, adam(wq[c], g * factor, qm[c], qs[c], RATE_MATRIX, WEIGHT_DECAY))
    put((om_new, os_new, o_new), ..., adam(wo[...], tail(second) * factor, om[...], os[...], RATE_OUT, WEIGHT_DECAY))
    for half in range(2):
        at = (slice(None), pl.ds(WIDE * half, WIDE))
        g = shards[0, 1 + half] * factor
        put((um_new, us_new, u_new), at, adam(wu[at], g, um[at], us[at], RATE_MATRIX, WEIGHT_DECAY))
        g = shards[1, 1 + half] * factor
        put((dm_new, ds_new, d_new), at, adam(wd[at], g, dm[at], ds[at], RATE_MATRIX, WEIGHT_DECAY))
    start = lax.axis_index("dp") * 24
    rolled = pltpu.roll(norm_sum[...], lax.rem(D - start, D), 1)
    g = rolled[0:4, 0:24] * factor
    norm_grad[...] = g
    put((nm_new, ns_new, n_new), ..., adam(norm[...], g, nm[...], ns[...], RATE_VECTOR, 0.0))
    stores = [pltpu.make_async_copy(src, dst, sem_out.at[k]) for k, (src, dst) in enumerate(zip(made, outs))]
    for store in stores:
        store.start()
    for came, leave in rows[4:]:
        came.wait()
        leave.start()
    for _, leave in rows:
        leave.wait()
    for store in stores:
        store.wait()


def step(out_in, grad_in, shards, norm_sum, square_sum, weights, moments):
    anywhere = pl.BlockSpec(memory_space=pl.ANY)
    like = lambda v: jax.ShapeDtypeStruct(v.shape, v.dtype)
    shapes = [like(out_in), like(grad_in), jax.ShapeDtypeStruct((1, 1), F32)]
    for w in weights:
        shapes += [like(w)] * 3
    shapes.append(like(weights[-1]))
    ins = (shards, norm_sum, square_sum, *weights, *moments)
    return pl.pallas_call(
        step_kernel,
        name="step",
        out_shape=shapes,
        in_specs=[anywhere] * 20,
        out_specs=[anywhere] * 19,
        scratch_shapes=[
            pltpu.VMEM((8, ROWS, D), BF),
            *[pltpu.VMEM(v.shape, v.dtype) for v in ins],
            *[pltpu.VMEM(v.shape, v.dtype) for v in shapes[2:]],
            pltpu.SemaphoreType.DMA((8,)),
            pltpu.SemaphoreType.DMA((8,)),
            pltpu.SemaphoreType.DMA((18,)),
            pltpu.SemaphoreType.DMA((17,)),
        ],
        compiler_params=pltpu.CompilerParams(vmem_limit_bytes=64 * 2**20),
    )(out_in, grad_in, *ins)


def body(
    tokens, time_emb, segments, cotangent, w_qkv, w_out, w_up, w_down, norm_params,
    qkv_first, qkv_second, out_first, out_second, up_first, up_second, down_first, down_second, norm_first, norm_second,
):
    weights = (w_qkv, w_out.T, w_up, w_down.T, norm_params)
    sent = layer(tokens, time_emb, segments, cotangent, *weights)
    moments = (
        qkv_first, qkv_second, out_first.T, out_second.T, up_first, up_second, down_first.T, down_second.T,
        norm_first, norm_second,
    )
    new = list(step(*sent, weights, moments))
    new[2] = new[2].reshape(())
    for k in (6, 7, 8, 12, 13, 14):
        new[k] = new[k].T
    return tuple(new)


def solution(mesh):
    return jax.shard_map(
        body,
        mesh=mesh,
        in_specs=(
            P("dp", None),
            P("dp", None),
            P("dp", None),
            P("dp", None),
            P(None, "dp", "mp"),
            P("mp", "dp"),
            P("dp", "mp"),
            P("mp", "dp"),
            P(None, "dp"),
            P(None, "dp", "mp"),
            P(None, "dp", "mp"),
            P("mp", "dp"),
            P("mp", "dp"),
            P("dp", "mp"),
            P("dp", "mp"),
            P("mp", "dp"),
            P("mp", "dp"),
            P(None, "dp"),
            P(None, "dp"),
        ),
        out_specs=(
            P("dp", None),
            P("dp", None),
            P(),
            P(None, "dp", "mp"),
            P(None, "dp", "mp"),
            P(None, "dp", "mp"),
            P("mp", "dp"),
            P("mp", "dp"),
            P("mp", "dp"),
            P("dp", "mp"),
            P("dp", "mp"),
            P("dp", "mp"),
            P("mp", "dp"),
            P("mp", "dp"),
            P("mp", "dp"),
            P(None, "dp"),
            P(None, "dp"),
            P(None, "dp"),
            P(None, "dp"),
        ),
        check_vma=False,
    )
```

```python
import jax
import jax.numpy as jnp
from jax import lax
from jax.experimental import pallas as pl
from jax.experimental.pallas import tpu as pltpu
from jax.sharding import PartitionSpec as P

MESH = pl.DeviceIdType.MESH

BF = jnp.bfloat16
F32 = jnp.float32
HEAD = 64
LEN = 128
ROWS = 512
D = 768
SEQS = 4
WIDE = 384
CLIP_AT = 1.0
BETA_ONE = 0.9
BETA_TWO = 0.95
ADAM_EPS = 1e-08
STEP = 10
WEIGHT_DECAY = 0.01
RATE_MATRIX = 0.05
RATE_OUT = 0.3
RATE_VECTOR = 0.5
GROUPS = 64
NORM_EPS = 1e-05


def nn(a, b):
    return jnp.dot(a, b, preferred_element_type=F32)


def nt(a, b):
    return lax.dot_general(a, b, (((1,), (1,)), ((), ())), preferred_element_type=F32)


def tn(a, b):
    return lax.dot_general(a, b, (((0,), (0,)), ((), ())), preferred_element_type=F32)


def whole(W, p, owner, zp):
    return W[p, owner, zp].reshape(D, D)


def columns(W, zp, base):
    return W[0, 1, zp, :, :, :, base : base + 256].reshape(D, 256)


def tiles(x):
    return x.astype(BF).reshape(4, 4, 48, x.shape[1])


def norm_stats(x):
    center = jnp.mean(x, axis=-1, keepdims=True)
    off = x - center
    inv = lax.rsqrt(jnp.mean(off * off, axis=-1, keepdims=True) + NORM_EPS)
    return off * inv, inv


def low_lanes(x):
    lane = lax.broadcasted_iota(jnp.int32, x.shape, x.ndim - 1)
    return lane < HEAD


def split_heads(x):
    first = low_lanes(x)
    zero = jnp.zeros_like(x)
    return jnp.concatenate([jnp.where(first, x, zero), jnp.where(first, zero, x)], axis=0)


def swap_halves(x):
    return pltpu.roll(x.astype(F32), HEAD, 1).astype(x.dtype)


def seq_rows(s):
    return pl.ds(pl.multiple_of(s * LEN, LEN), LEN)


def first_norm(place, tok, time, gains, segs, xs, n1, bias):
    for s in range(SEQS):
        rows = slice(s * LEN, s * LEN + LEN)
        x = tok[rows, :].astype(F32) + time[pl.ds(SEQS * place + s, 1), :]
        xs[rows, :] = x
        scaled, _ = norm_stats(x)
        n1[rows, :] = (scaled * gains[0:1, :] + gains[1:2, :]).astype(BF)
        lab = jnp.broadcast_to(segs[pl.ds(SEQS * place + s, 1), :].astype(F32), (LEN, LEN))
        bias[s] = jnp.where(lab == lab.T, 0.0, -1e30).astype(F32)


def project(h, n1, W, pq, pv):
    rows = slice(256 * h, 256 * h + 256)
    for zp in range(2):
        pq[zp, rows, :] = nn(n1[rows, :], whole(W, 0, 0, zp)).astype(BF)
        for j in range(2):
            pv[2 * zp + j, rows, :] = nn(n1[rows, :], columns(W, zp, 384 * j)).astype(BF)


def softmax_columns(scores):
    e = jnp.exp(scores - jnp.max(scores, axis=1, keepdims=True))
    return (e * (1.0 / jnp.sum(e, axis=1, keepdims=True))).astype(BF)


def value_two(vg):
    first = low_lanes(vg)
    return swap_halves(jnp.where(first, vg, jnp.zeros_like(vg)))


def attention(lo, hi, pq, pv, bias, probs, mx):
    scaling = HEAD ** (-0.5)

    def step(i, _):
        s, zp = i // 2, i % 2
        rows = seq_rows(s)
        mask = bias[s]
        for j in range(2):
            z = 2 * zp + j
            base = 384 * j
            ga = pq[zp, rows, base : base + 128]
            gb = pq[zp, rows, base + 128 : base + 256]
            gc = pq[zp, rows, base + 256 : base + 384]
            va = pv[z, rows, 0:128]
            vb = value_two(pv[z, rows, 128:256])
            both = swap_halves(gb)
            first = low_lanes(gb)
            s01 = nt(split_heads(gc), ga)
            s2 = nt(jnp.where(first, both, jnp.zeros_like(gb)), gb)
            scores = jnp.concatenate([s01, s2], axis=0).reshape(3, LEN, LEN)
            p = softmax_columns(scores * scaling + mask[None]).reshape(3 * LEN, LEN)
            probs[s, z] = p
            mx[z, rows, 128:256] = tn(p[: 2 * LEN], split_heads(va)).astype(BF)
            mx[z, rows, 0:128] = tn(p[2 * LEN :], vb).astype(BF)
        return 0

    lax.fori_loop(lo, hi, step, 0, unroll=4)


def second_norm(h, W, mx, xs, gains, mid, n2):
    rows = slice(256 * h, 256 * h + 256)
    acc = xs[rows, :]
    for z in range(4):
        base = 384 * (z % 2) + 128
        acc = acc + nt(mx[z, rows, :], columns(W, z // 2, base))
    mid[rows, :] = acc
    scaled, _ = norm_stats(acc)
    n2[rows, :] = (scaled * gains[2:3, :] + gains[3:4, :]).astype(BF)


def gelu_parts(u):
    cdf = 0.5 * (1.0 + lax.erf(u * 0.7071067811865476))
    pdf = jnp.exp(u * u * -0.5) * 0.3989422804014327
    return u * cdf, cdf + u * pdf


def feed_out(h, p, zp, W, n2, act, slope, acc_out):
    at = 2 * (p - 1) + zp
    rows = slice(256 * h, 256 * h + 256)
    a, rate = gelu_parts(nn(n2[rows, :], whole(W, p, 0, zp)))
    a = a.astype(BF)
    act[at, rows, :] = a
    slope[at, rows, :] = rate.astype(BF)
    out = nt(a, whole(W, p, 1, zp))
    if at == 0:
        acc_out[rows, :] = out
    else:
        acc_out[rows, :] += out


def layer_rows(h, mid, acc_out, rows_out):
    rows = slice(256 * h, 256 * h + 256)
    rows_out[rows, :] = (mid[rows, :] + acc_out[rows, :]).astype(BF)


def feed_back(p, zp, W, ct, slope, acc_g):
    at = 2 * (p - 1) + zp
    for h in range(2):
        rows = slice(256 * h, 256 * h + 256)
        slope[at, rows, :] = (nn(ct[rows, :], whole(W, p, 1, zp)) * slope[at, rows, :].astype(F32)).astype(BF)
    back = nt(slope[at], whole(W, p, 0, zp))
    if at == 0:
        acc_g[...] = back
    else:
        acc_g[...] += back


def feed_grads(p, zp, G, n2, ct, act, slope):
    at = 2 * (p - 1) + zp
    G[p, 1, zp] = tiles(tn(ct[...], act[at]))
    G[p, 0, zp] = tiles(tn(n2[...], slope[at]))


def norm_back(grad, scaled, inv, gain):
    u = grad * gain
    m1 = jnp.mean(u, axis=-1, keepdims=True)
    m2 = jnp.mean(u * scaled, axis=-1, keepdims=True)
    return inv * (u - m1 - scaled * m2)


def second_back(mid, acc_g, ct, gains, br, ng):
    ng[4:8, :] = jnp.zeros((4, D), F32)
    scaled, inv = norm_stats(mid[...])
    g = acc_g[...]
    ng[2:3, :] = jnp.sum(g * scaled, axis=0, keepdims=True)
    ng[3:4, :] = jnp.sum(g, axis=0, keepdims=True)
    gm = ct[...].astype(F32) + norm_back(g, scaled, inv, gains[2:3, :])
    mid[...] = gm
    br[...] = gm.astype(BF)


def mixed_grad(W, br, dm):
    for z in range(4):
        base = 384 * (z % 2) + 128
        dm[z // 2, :, base - 128 : base + 128] = nn(br[...], columns(W, z // 2, base)).astype(BF)


def attention_back(lo, hi, zp, pq, pv, probs, dm, dpq, dpv):
    scaling = HEAD ** (-0.5)

    def step(s, _):
        rows = seq_rows(s)
        for j in range(2):
            z = 2 * zp + j
            base = 384 * j
            ga = pq[zp, rows, base : base + 128]
            gb = pq[zp, rows, base + 128 : base + 256]
            gc = pq[zp, rows, base + 256 : base + 384]
            va = pv[z, rows, 0:128]
            vb = value_two(pv[z, rows, 128:256])
            p = probs[s, z]
            db = dm[zp, rows, base : base + 128]
            da = dm[zp, rows, base + 128 : base + 256]
            gp = jnp.concatenate([nt(split_heads(va), da), nt(vb, db)], axis=0).reshape(3, LEN, LEN)
            pf = p.astype(F32).reshape(3, LEN, LEN)
            ds = (pf * (gp - jnp.sum(gp * pf, axis=1, keepdims=True))).astype(BF).reshape(3 * LEN, LEN)
            beside = lambda v: jnp.concatenate([v[:LEN], v[LEN : 2 * LEN]], axis=1)
            dv01 = nn(beside(p), split_heads(da))
            dk01 = nn(beside(ds), split_heads(ga)) * scaling
            dq01 = tn(ds[: 2 * LEN], split_heads(gc)) * scaling
            dv2 = pltpu.roll(nn(p[2 * LEN :], db), HEAD, 1)
            both = swap_halves(gb)
            dk2 = nn(ds[2 * LEN :], both)
            dq2 = tn(ds[2 * LEN :], both)
            first = low_lanes(dq2)
            dpq[zp, rows, base : base + 128] = dq01.astype(BF)
            dpq[zp, rows, base + 128 : base + 256] = (jnp.where(first, dq2, dk2) * scaling).astype(BF)
            dpq[zp, rows, base + 256 : base + 384] = dk01.astype(BF)
            dpv[2 + zp, rows, base : base + 128] = dv01.astype(BF)
            dpv[2 + zp, rows, base + 128 : base + 256] = jnp.where(first, dv2, 0.0).astype(BF)
        return 0

    lax.fori_loop(lo, hi, step, 0, unroll=2)


def input_grad_sum(W, dpq, dpv, gn):
    acc = nt(dpq[0], whole(W, 0, 0, 0)) + nt(dpq[1], whole(W, 0, 0, 1))
    for z in range(4):
        acc = acc + nt(dpv[2 + z // 2, :, 384 * (z % 2) : 384 * (z % 2) + 256], columns(W, z // 2, 384 * (z % 2)))
    gn[...] = acc


def first_grads(zp, G, n1, br, mx, dpq, dpv):
    G[0, 0, zp] = tiles(tn(n1[...], dpq[zp]))
    for j in range(2):
        z = 2 * zp + j
        base = 384 * j
        gv = tn(n1[...], dpv[2 + zp, :, base : base + 256])
        go = tn(br[...], mx[z])
        G[0, 1, zp, :, :, :, base : base + 128] = tiles(gv[:, :128])
        G[0, 1, zp, :, :, :, base + 128 : base + 256] = tiles(gv[:, 128:] + go[:, :128])
        G[0, 1, zp, :, :, :, base + 256 : base + 384] = tiles(go[:, 128:])


def first_back(h, xs, gn, mid, gains, ng, dx):
    rows = slice(256 * h, 256 * h + 256)
    scaled, inv = norm_stats(xs[rows, :])
    g = gn[rows, :]
    gain = jnp.sum(g * scaled, axis=0, keepdims=True)
    shift = jnp.sum(g, axis=0, keepdims=True)
    if h == 0:
        ng[0:1, :] = gain
        ng[1:2, :] = shift
    else:
        ng[0:1, :] += gain
        ng[1:2, :] += shift
    dx[rows, :] = (mid[rows, :] + norm_back(g, scaled, inv, gains[0:1, :])).astype(BF)


class Place:
    def __init__(self):
        dp = lax.axis_index("dp")
        self.dp = dp
        self.at = {"z": lax.axis_index("mp"), "y": dp // 8, "x": (dp // 2) % 4, "c": dp % 2}

    def step(self, axis, d):
        return (self.at[axis] + d) % (2 if axis == "c" else 4)

    def device(self, **moves):
        q = {axis: self.step(axis, moves.get(axis, 0)) for axis in self.at}
        return ((q["y"] * 4 + q["x"]) * 2 + q["c"], q["z"])


NEAR = [{axis: d} for axis in ("x", "y", "z") for d in (1, 2, 3)] + [{"c": 1}]


class Net:
    def __init__(self, place, send_sem, recv_sem):
        self.place, self.send_sem, self.recv_sem = place, send_sem, recv_sem
        self.groups = []

    def group(self, like):
        group = Group(self, len(self.groups), like)
        self.groups.append(group)
        return group

    def finish(self):
        for group in self.groups:
            group.every.wait_send()


class Group:
    def __init__(self, net, k, like):
        self.net, self.k = net, k
        self.every = self.copy(like, like, net.place.device(c=1))

    def copy(self, src, dst, to):
        return pltpu.make_async_remote_copy(
            src_ref=src,
            dst_ref=dst,
            send_sem=self.net.send_sem.at[self.k],
            recv_sem=self.net.recv_sem.at[self.k],
            device_id=to,
            device_id_type=MESH,
        )

    def push(self, src, dst, axis, d):
        self.copy(src, dst, self.net.place.device(**{axis: d})).start()

    def arrive(self):
        self.every.wait_recv()


def lanes(z):
    return pl.ds(pl.multiple_of((z % 2) * WIDE, 128), WIDE)


def weight_view(W, p, owner, r, at):
    y = slice(None) if at["y"] is None else at["y"]
    x = slice(None) if at["x"] is None else at["x"]
    rows = pl.ds(16 * r, 16)
    if at["z"] is None:
        return W.at[p, owner, :, y, x, rows, :]
    return W.at[p, owner, at["z"] // 2, y, x, rows, lanes(at["z"])]


ORDERS = (("x", "y", "z"), ("y", "z", "x"), ("z", "x", "y"))


class Gather:
    def __init__(self, net, W, p):
        self.net, self.W, self.p = net, W, p
        self.core = net.place.at["c"]
        self.across = net.group(W.at[p, self.core])

    def view(self, r, at):
        return weight_view(self.W, self.p, self.core, r, at)

    def known(self, r, done, **moved):
        at = dict(self.net.place.at)
        for axis in ORDERS[r][:done]:
            at[axis] = None
        at.update(moved)
        return at

    def spread(self, done, ds, like):
        self.step = self.net.group(like)
        for r in range(3):
            src = self.view(r, self.known(r, done))
            for d in ds:
                self.step.push(src, src, ORDERS[r][done], d)

    def share(self, r, at):
        src = self.view(r, at)
        self.across.push(src, src, "c", 1)

    def first(self):
        self.spread(0, (1, 3, 2), self.W.at[self.p, self.core, 0, 0, 0:3, :, 0:WIDE])

    def second(self):
        self.step.arrive()
        self.spread(1, (1, 3, 2), self.W.at[self.p, self.core, 0, :, 0:3, :, 0:WIDE])

    def third(self):
        self.step.arrive()
        self.spread(2, (1, 3), self.W.at[self.p, self.core, 0])
        for r in range(3):
            self.share(r, self.known(r, 2))

    def fourth(self):
        self.step.arrive()
        self.step = self.net.group(self.W.at[self.p, self.core, 0, :, :, :, 0:WIDE])
        for r in range(3):
            axis = ORDERS[r][2]
            cut = "x" if axis == "y" else "y"
            for side, d in ((0, 1), (1, 3)):
                half = {axis: self.net.place.step(axis, -d), cut: pl.ds(2 * side, 2)}
                src = self.view(r, self.known(r, 2, **half))
                self.step.push(src, src, axis, d)
        for r in range(3):
            axis = ORDERS[r][2]
            for d in (3, 1):
                self.share(r, self.known(r, 2, **{axis: self.net.place.step(axis, d)}))

    def fifth(self):
        self.step.arrive()
        for r in range(3):
            axis = ORDERS[r][2]
            self.share(r, self.known(r, 2, **{axis: self.net.place.step(axis, 2)}))

    def last(self):
        self.across.arrive()


class Scatter:
    def __init__(self, net, G, p, zp, slot, cross, half, full, small):
        self.net, self.G, self.p, self.zp, self.slot = net, G, p, zp, slot
        self.cross, self.half, self.full, self.small = cross, half, full, small
        self.core = net.place.at["c"]

    def view(self, j, y, x):
        return (self.p, self.core, self.zp, y, x, slice(None), pl.ds(WIDE * j, WIDE))

    def block(self, j, d, cut=slice(None)):
        if j == 0:
            return self.view(0, cut, self.net.place.step("x", d))
        return self.view(1, self.net.place.step("y", d), cut)

    def own(self, j, d):
        at = self.net.place.at
        if j == 0:
            return self.view(0, self.net.place.step("y", d), at["x"])
        return self.view(1, at["y"], self.net.place.step("x", d))

    def to_core(self):
        dst = self.cross.at[self.slot]
        self.step = self.net.group(dst)
        self.step.push(self.G.at[self.p, 1 - self.core, self.zp], dst, "c", 1)

    def add_core(self):
        self.step.arrive()

        def per_y(y, _):
            at = (self.p, self.core, self.zp, y)
            self.G[at] = self.G[at] + self.cross[self.slot, y]
            return 0

        lax.fori_loop(0, 4, per_y, 0)
        self.step = self.net.group(self.half.at[self.slot])
        for side, d in ((0, 1), (1, 3)):
            for j, axis in ((0, "x"), (1, "y")):
                src = self.G.at[self.block(j, 2, pl.ds(2 * side, 2))]
                self.step.push(src, self.half.at[self.slot, j, side], axis, d)

    def add_half(self):
        self.step.arrive()
        self.step = self.net.group(self.full.at[self.p, self.zp])
        for side, d in ((0, 1), (1, 3)):
            for j, axis in ((0, "x"), (1, "y")):
                at = self.block(j, d, pl.ds(2 * side, 2))
                self.G[at] = self.G[at] + self.half[self.slot, j, side]
                self.step.push(self.G.at[self.block(j, d)], self.full.at[self.p, self.zp, j, side], axis, d)

    def add_full(self):
        self.step.arrive()
        self.step = self.net.group(self.small.at[self.p, self.zp])
        for j, axis in ((0, "y"), (1, "x")):
            at = self.block(j, 0)
            total = self.G[at].astype(F32)
            for side in range(2):
                total = total + self.full[self.p, self.zp, j, side].astype(F32)
            self.G[at] = total.astype(BF)
            for d in (1, 3, 2):
                self.step.push(self.G.at[self.own(j, d)], self.small.at[self.p, self.zp, j, d - 1], axis, d)

    def add_small(self):
        self.step.arrive()
        for j in range(2):
            at = self.own(j, 0)
            total = self.G[at].astype(F32)
            for d in range(3):
                total = total + self.small[self.p, self.zp, j, d].astype(F32)
            self.G[at] = total.astype(BF)


class Deep:
    def __init__(self, net, G, p, tiny, done):
        self.net, self.G, self.p, self.tiny, self.done = net, G, p, tiny, done

    def chunk(self, d):
        at = self.net.place.at
        z = self.net.place.step("z", d)
        return (self.p, at["c"], z // 2, at["y"], at["x"], slice(None), lanes(z))

    def send(self):
        self.step = self.net.group(self.tiny.at[self.p])
        for d in (1, 3, 2):
            self.step.push(self.G.at[self.chunk(d)], self.tiny.at[self.p, d - 1], "z", d)

    def add(self):
        self.step.arrive()
        total = self.G[self.chunk(0)].astype(F32)
        for d in range(3):
            total = total + self.tiny[self.p, d].astype(F32)
        self.done[self.p] = total
        return jnp.sum(total * total)


class Sum:
    def __init__(self, net, slots):
        self.net, self.slots = net, slots

    def send(self, axis, value):
        slots = self.slots[axis]
        here = self.net.place.at[axis]
        self.axis = axis
        slots[here] = value
        ds = (1,) if axis == "c" else (1, 3, 2)
        self.step = self.net.group(slots.at[0 : len(ds)])
        for d in ds:
            self.step.push(slots.at[here], slots.at[here], axis, d)

    def add(self):
        self.step.arrive()
        slots = self.slots[self.axis]
        total = slots[0]
        for k in range(1, slots.shape[0]):
            total = total + slots[k]
        return total


class Rows:
    def __init__(self, net, rows_ref, out, sem):
        self.net, self.rows_ref, self.out, self.sem = net, rows_ref, out, sem
        self.near, self.local = [], []
        self.far = net.group(out.at[0:ROWS, :])

    def place_of(self, d, piece, side=None):
        start = ROWS * self.net.place.step("z", d) + 256 * piece
        if side is None:
            return self.out.at[pl.ds(pl.multiple_of(start, 256), 256), :]
        return self.out.at[pl.ds(pl.multiple_of(start + 128 * side, 128), 128), :]

    def send(self, piece):
        src = self.rows_ref.at[pl.ds(256 * piece, 256), :]
        near = self.net.group(self.out.at[0:ROWS, :])
        self.near.append(near)
        for d in (1, 3):
            near.push(src, self.place_of(0, piece), "z", d)
        self.local.append(pltpu.make_async_copy(src, self.place_of(0, piece), self.sem.at[piece]))
        self.local[piece].start()

    def forward(self, piece):
        self.near[piece].arrive()
        for side, d in ((0, 1), (1, 3)):
            src = self.place_of(-d, piece, side)
            self.far.push(src, src, "z", d)

    def finish(self):
        self.far.arrive()
        for copy in self.local:
            copy.wait()


def pack(wq, wo, wu, wd, keep):
    q, k, v, o = wq[0], wq[1], wq[2], wo[...]
    keep[0, 0] = jnp.concatenate([q, k[:, 128:], k[:, :128]], axis=1)
    keep[1, 0] = jnp.concatenate([v, o[:, 128:], o[:, :128]], axis=1)
    for half in range(2):
        keep[0, 1 + half] = wu[:, WIDE * half : WIDE * half + WIDE]
        keep[1, 1 + half] = wd[:, WIDE * half : WIDE * half + WIDE]


def layer_kernel(
    tokens, time_in, segs_in, cotangent, wq_in, wo_in, wu_in, wd_in, norm_in,
    out, input_grad, shards, norm_sum, square_sum,
    W, G, cross, half, full, small, tiny, done, keep, other,
    gx, gy, gc, nx, ny, nz, nc, sx, sy, sz, sc, gains, time, ng,
    xs, n1, bias, pq, pv, probs, mx, mid, n2, act, slope, acc_g, tok, ct,
    time_emb, segs, wq, wo, wu, wd, norm,
    send_sem, recv_sem, local_sem, out_sem, in_sem, free_sem,
):
    place = Place()
    net = Net(place, send_sem, recv_sem)
    z, core = place.at["z"], place.at["c"]
    mine = pl.ds(pl.multiple_of(ROWS * z, ROWS), ROWS)
    pairs = (
        (wq_in, wq), (wo_in, wo), (wu_in, wu), (wd_in, wd), (norm_in, norm),
        (time_in, time_emb), (segs_in, segs), (tokens.at[mine, :], tok), (cotangent.at[mine, :], ct),
    )
    loads = [pltpu.make_async_copy(src, dst, local_sem.at[i]) for i, (src, dst) in enumerate(pairs)]
    for load in loads:
        load.start()
    barrier = pltpu.get_barrier_semaphore()
    for moves in NEAR:
        pl.semaphore_signal(barrier, inc=1, device_id=place.device(**moves), device_id_type=MESH)
    for load in loads[:5]:
        load.wait()
    pack(wq, wo, wu, wd, keep)
    column = lax.broadcasted_iota(jnp.int32, (24, D), 1)
    row = lax.broadcasted_iota(jnp.int32, (24, D), 0)
    spot = jnp.where(column == row + 24 * place.dp, 1.0, 0.0).astype(F32)
    rounded = norm[...].astype(BF).astype(F32)
    spread = jnp.concatenate([nn(rounded, spot), jnp.zeros((4, D), F32)], axis=0)
    pl.semaphore_wait(barrier, len(NEAR))

    swap = net.group(other)
    swap.push(keep.at[1 - core], other, "c", 1)
    gain_sum = Sum(net, {"x": gx, "y": gy, "c": gc})
    gain_sum.send("x", spread)
    swap.arrive()
    for p in range(3):
        kept = keep[core, p]
        came = other[p]
        even = core == 0
        rows = jnp.concatenate([jnp.where(even, kept, came), jnp.where(even, came, kept)], axis=0)
        W[p, core, z // 2, place.at["y"], place.at["x"], :, lanes(z)] = rows.astype(BF)
    parts = [Gather(net, W, p) for p in range(3)]
    for part in parts:
        part.first()
    gain_sum.send("y", gain_sum.add())
    parts[0].second()
    parts[1].second()
    gain_sum.send("c", gain_sum.add())
    parts[0].third()
    parts[2].second()
    for load in loads[5:]:
        load.wait()
    time[...] = time_emb[...].astype(F32)
    gains[...] = gain_sum.add()
    parts[0].fourth()
    parts[1].third()
    parts[2].third()
    first_norm(z, tok, time, gains, segs, xs, n1, bias)
    parts[0].fifth()
    parts[0].last()

    out_rows = Rows(net, tok, out, out_sem)
    in_rows = Rows(net, pq.at[0], input_grad, in_sem)
    norm_total = Sum(net, {"c": nc, "x": nx, "y": ny, "z": nz})
    units = ((1, 0), (1, 1), (2, 0), (2, 1), (0, 0), (0, 1))
    sums = [Scatter(net, G, p, zp, 2 * max(p - 1, 0) + zp, cross, half, full, small) for p, zp in units]
    deep = [Deep(net, G, p, tiny, done) for p in range(3)]
    squares = [None] * 3

    def free():
        pl.semaphore_signal(free_sem, inc=1, device_id=place.device(c=1), device_id_type=MESH)

    project(0, n1, W, pq, pv)
    parts[1].fourth()
    attention(0, 4, pq, pv, bias, probs, mx)
    parts[2].fourth()
    project(1, n1, W, pq, pv)
    parts[1].fifth()
    attention(4, 8, pq, pv, bias, probs, mx)
    parts[2].fifth()
    second_norm(0, W, mx, xs, gains, mid, n2)
    second_norm(1, W, mx, xs, gains, mid, n2)
    parts[1].last()
    feed_out(0, 1, 0, W, n2, act, slope, acc_g)
    feed_out(0, 1, 1, W, n2, act, slope, acc_g)
    parts[2].last()
    feed_out(0, 2, 0, W, n2, act, slope, acc_g)
    feed_out(0, 2, 1, W, n2, act, slope, acc_g)
    layer_rows(0, mid, acc_g, tok)
    out_rows.send(0)
    feed_out(1, 1, 0, W, n2, act, slope, acc_g)
    feed_out(1, 1, 1, W, n2, act, slope, acc_g)
    feed_out(1, 2, 0, W, n2, act, slope, acc_g)
    feed_out(1, 2, 1, W, n2, act, slope, acc_g)
    layer_rows(1, mid, acc_g, tok)
    out_rows.send(1)
    feed_back(1, 0, W, ct, slope, acc_g)
    feed_grads(1, 0, G, n2, ct, act, slope)
    sums[0].to_core()
    feed_back(1, 1, W, ct, slope, acc_g)
    feed_grads(1, 1, G, n2, ct, act, slope)
    sums[1].to_core()
    feed_back(2, 0, W, ct, slope, acc_g)
    sums[0].add_core()
    free()
    feed_grads(2, 0, G, n2, ct, act, slope)
    sums[2].to_core()
    feed_back(2, 1, W, ct, slope, acc_g)
    out_rows.forward(0)
    sums[1].add_core()
    free()
    feed_grads(2, 1, G, n2, ct, act, slope)
    sums[3].to_core()
    sums[0].add_half()
    sums[2].add_core()
    second_back(mid, acc_g, ct, gains, n2, ng)
    mixed_grad(W, n2, slope)
    attention_back(0, 2, 0, pq, pv, probs, slope, act, slope)
    sums[1].add_half()
    sums[3].add_core()
    attention_back(2, 4, 0, pq, pv, probs, slope, act, slope)
    first_grads(0, G, n1, n2, mx, act, slope)
    pl.semaphore_wait(free_sem, 1)
    sums[4].to_core()
    sums[0].add_full()
    out_rows.forward(1)
    attention_back(0, 2, 1, pq, pv, probs, slope, act, slope)
    sums[2].add_half()
    attention_back(2, 4, 1, pq, pv, probs, slope, act, slope)
    sums[4].add_core()
    sums[1].add_full()
    first_grads(1, G, n1, n2, mx, act, slope)
    pl.semaphore_wait(free_sem, 1)
    sums[5].to_core()
    sums[3].add_half()
    input_grad_sum(W, act, slope, acc_g)
    sums[0].add_small()
    first_back(0, xs, acc_g, mid, gains, ng, pq.at[0])
    in_rows.send(0)
    first_back(1, xs, acc_g, mid, gains, ng, pq.at[0])
    in_rows.send(1)
    norm_total.send("c", ng[...])
    sums[5].add_core()
    sums[2].add_full()
    sums[4].add_half()
    sums[1].add_small()
    deep[1].send()
    norm_total.send("x", norm_total.add())
    sums[3].add_full()
    sums[5].add_half()
    sums[2].add_small()
    sums[4].add_full()
    sums[3].add_small()
    deep[2].send()
    norm_total.send("y", norm_total.add())
    sums[5].add_full()
    sums[4].add_small()
    norm_total.send("z", norm_total.add())
    sums[5].add_small()
    deep[0].send()
    in_rows.forward(0)
    in_rows.forward(1)
    squares[1] = deep[1].add()
    norm_rows = norm_total.add()
    squares[2] = deep[2].add()
    squares[0] = deep[0].add()
    norm_sum[...] = norm_rows
    other_rows = pl.ds(pl.multiple_of(24 * (1 - core), 8), 24)
    own_rows = pl.ds(pl.multiple_of(24 * core, 8), 24)
    trade = net.group(shards.at[core])
    trade.push(done.at[:, other_rows, :], shards.at[core], "c", 1)
    total = Sum(net, {"c": sc, "x": sx, "y": sy, "z": sz})
    total.send("c", jnp.full((8, 128), squares[0] + squares[1] + squares[2], F32))
    shards[core] = done[:, own_rows, :]
    total.send("x", total.add())
    total.send("y", total.add())
    total.send("z", total.add())
    square_sum[...] = total.add() + jnp.sum(norm_rows * norm_rows)
    trade.arrive()
    out_rows.finish()
    in_rows.finish()
    net.finish()


def layer(tokens, time_emb, segs, cotangent, wq, wo, wu, wd, norm):
    V = pltpu.VMEM
    rows, low = (ROWS, D), BF
    anywhere = pl.BlockSpec(memory_space=pl.ANY)
    near = pl.BlockSpec(memory_space=pltpu.VMEM)
    return pl.pallas_call(
        layer_kernel,
        name="layer",
        out_shape=(
            jax.ShapeDtypeStruct(tokens.shape, BF),
            jax.ShapeDtypeStruct(tokens.shape, BF),
            jax.ShapeDtypeStruct((2, 3, 24, WIDE), F32),
            jax.ShapeDtypeStruct((8, D), F32),
            jax.ShapeDtypeStruct((8, 128), F32),
        ),
        in_specs=[anywhere] * 9,
        out_specs=[anywhere, anywhere, near, near, near],
        scratch_shapes=[
            V((3, 2, 2, 4, 4, 48, D), low),
            V((3, 2, 2, 4, 4, 48, D), low),
            V((4, 4, 4, 48, D), low),
            V((4, 2, 2, 2, 48, WIDE), low),
            V((3, 2, 2, 2, 4, 48, WIDE), low),
            V((3, 2, 2, 3, 48, WIDE), low),
            V((3, 3, 48, WIDE), low),
            V((3, 48, WIDE), F32),
            V((2, 3, 24, WIDE), F32),
            V((3, 24, WIDE), F32),
            V((4, 8, D), F32),
            V((4, 8, D), F32),
            V((2, 8, D), F32),
            V((4, 8, D), F32),
            V((4, 8, D), F32),
            V((4, 8, D), F32),
            V((2, 8, D), F32),
            V((4, 8, 128), F32),
            V((4, 8, 128), F32),
            V((4, 8, 128), F32),
            V((2, 8, 128), F32),
            V((8, D), F32),
            V((16, D), F32),
            V((8, D), F32),
            V(rows, F32),
            V(rows, low),
            V((SEQS, LEN, LEN), F32),
            V((2, ROWS, D), low),
            V((4, ROWS, 256), low),
            V((SEQS, 4, WIDE, LEN), low),
            V((4, ROWS, 256), low),
            V(rows, F32),
            V(rows, low),
            V((4, ROWS, D), low),
            V((4, ROWS, D), low),
            V(rows, F32),
            V(rows, low),
            V(rows, low),
            V(time_emb.shape, low),
            V(segs.shape, jnp.int32),
            V(wq.shape, F32),
            V(wo.shape, F32),
            V(wu.shape, F32),
            V(wd.shape, F32),
            V(norm.shape, F32),
            pltpu.SemaphoreType.DMA((GROUPS,)),
            pltpu.SemaphoreType.DMA((GROUPS,)),
            pltpu.SemaphoreType.DMA((9,)),
            pltpu.SemaphoreType.DMA((2,)),
            pltpu.SemaphoreType.DMA((2,)),
            pltpu.SemaphoreType.REGULAR,
        ],
        compiler_params=pltpu.CompilerParams(
            collective_id=0, has_side_effects=True, vmem_limit_bytes=64 * 2**20
        ),
    )(tokens, time_emb, segs, cotangent, wq, wo, wu, wd, norm)


def adam(weight, gradient, moment, second, step_rate, decay_rate):
    moment = BETA_ONE * moment + (1.0 - BETA_ONE) * gradient
    second = BETA_TWO * second + (1.0 - BETA_TWO) * gradient * gradient
    moment_hat = moment / (1.0 - BETA_ONE**STEP)
    second_hat = second / (1.0 - BETA_TWO**STEP)
    weight = weight - step_rate * (
        moment_hat / (jnp.sqrt(second_hat) + ADAM_EPS) + decay_rate * weight
    )
    return (moment, second, weight)


def step_kernel(*refs):
    out_in, grad_in, *ins = refs[:20]
    out, grad, *outs = refs[20:39]
    held, kept, made, row_in, row_out, sem_in, sem_out = refs[39], refs[40:58], refs[58:75], *refs[75:]
    loads = [pltpu.make_async_copy(src, dst, sem_in.at[k]) for k, (src, dst) in enumerate(zip(ins, kept))]
    rows = []
    for k in range(8):
        at = pl.ds(ROWS * (k % 4), ROWS)
        src, dst = ((out_in, out), (grad_in, grad))[k // 4]
        rows.append(
            (
                pltpu.make_async_copy(src.at[at, :], held.at[k], row_in.at[k]),
                pltpu.make_async_copy(held.at[k], dst.at[at, :], row_out.at[k]),
            )
        )
    for load in loads:
        load.start()
    for came, _ in rows:
        came.start()
    for load in loads:
        load.wait()
    for came, leave in rows[:4]:
        came.wait()
        leave.start()
    shards, norm_sum, square_sum, wq, wo, wu, wd, norm, qm, qs, om, os, um, us, dm, ds, nm, ns = kept
    total, qm_new, qs_new, q_new, om_new, os_new, o_new, um_new, us_new, u_new = made[:10]
    dm_new, ds_new, d_new, nm_new, ns_new, n_new, norm_grad = made[10:]
    grad_norm = jnp.sqrt(square_sum[0:1, 0:1])
    total[...] = grad_norm
    factor = jnp.minimum(1.0, CLIP_AT / (grad_norm + 1e-06))

    def put(refs, at, value):
        for ref, new in zip(refs, value):
            ref[at] = new

    first, second = shards[0, 0], shards[1, 0]
    tail = lambda v: jnp.concatenate([v[:, 256:], v[:, 192:256]], axis=1)
    for c, g in enumerate((first[:, :192], tail(first), second[:, :192])):
        put((qm_new, qs_new, q_new), c, adam(wq[c], g * factor, qm[c], qs[c], RATE_MATRIX, WEIGHT_DECAY))
    put((om_new, os_new, o_new), ..., adam(wo[...], tail(second) * factor, om[...], os[...], RATE_OUT, WEIGHT_DECAY))
    for half in range(2):
        at = (slice(None), pl.ds(WIDE * half, WIDE))
        g = shards[0, 1 + half] * factor
        put((um_new, us_new, u_new), at, adam(wu[at], g, um[at], us[at], RATE_MATRIX, WEIGHT_DECAY))
        g = shards[1, 1 + half] * factor
        put((dm_new, ds_new, d_new), at, adam(wd[at], g, dm[at], ds[at], RATE_MATRIX, WEIGHT_DECAY))
    start = lax.axis_index("dp") * 24
    rolled = pltpu.roll(norm_sum[...], lax.rem(D - start, D), 1)
    g = rolled[0:4, 0:24] * factor
    norm_grad[...] = g
    put((nm_new, ns_new, n_new), ..., adam(norm[...], g, nm[...], ns[...], RATE_VECTOR, 0.0))
    stores = [pltpu.make_async_copy(src, dst, sem_out.at[k]) for k, (src, dst) in enumerate(zip(made, outs))]
    for store in stores:
        store.start()
    for came, leave in rows[4:]:
        came.wait()
        leave.start()
    for _, leave in rows:
        leave.wait()
    for store in stores:
        store.wait()


def step(out_in, grad_in, shards, norm_sum, square_sum, weights, moments):
    anywhere = pl.BlockSpec(memory_space=pl.ANY)
    like = lambda v: jax.ShapeDtypeStruct(v.shape, v.dtype)
    shapes = [like(out_in), like(grad_in), jax.ShapeDtypeStruct((1, 1), F32)]
    for w in weights:
        shapes += [like(w)] * 3
    shapes.append(like(weights[-1]))
    ins = (shards, norm_sum, square_sum, *weights, *moments)
    return pl.pallas_call(
        step_kernel,
        name="step",
        out_shape=shapes,
        in_specs=[anywhere] * 20,
        out_specs=[anywhere] * 19,
        scratch_shapes=[
            pltpu.VMEM((8, ROWS, D), BF),
            *[pltpu.VMEM(v.shape, v.dtype) for v in ins],
            *[pltpu.VMEM(v.shape, v.dtype) for v in shapes[2:]],
            pltpu.SemaphoreType.DMA((8,)),
            pltpu.SemaphoreType.DMA((8,)),
            pltpu.SemaphoreType.DMA((18,)),
            pltpu.SemaphoreType.DMA((17,)),
        ],
        compiler_params=pltpu.CompilerParams(vmem_limit_bytes=64 * 2**20),
    )(out_in, grad_in, *ins)


def body(
    tokens, time_emb, segments, cotangent, w_qkv, w_out, w_up, w_down, norm_params,
    qkv_first, qkv_second, out_first, out_second, up_first, up_second, down_first, down_second, norm_first, norm_second,
):
    weights = (w_qkv, w_out.T, w_up, w_down.T, norm_params)
    sent = layer(tokens, time_emb, segments, cotangent, *weights)
    moments = (
        qkv_first, qkv_second, out_first.T, out_second.T, up_first, up_second, down_first.T, down_second.T,
        norm_first, norm_second,
    )
    new = list(step(*sent, weights, moments))
    new[2] = new[2].reshape(())
    for k in (6, 7, 8, 12, 13, 14):
        new[k] = new[k].T
    return tuple(new)


def solution(mesh):
    return jax.shard_map(
        body,
        mesh=mesh,
        in_specs=(
            P("dp", None),
            P("dp", None),
            P("dp", None),
            P("dp", None),
            P(None, "dp", "mp"),
            P("mp", "dp"),
            P("dp", "mp"),
            P("mp", "dp"),
            P(None, "dp"),
            P(None, "dp", "mp"),
            P(None, "dp", "mp"),
            P("mp", "dp"),
            P("mp", "dp"),
            P("dp", "mp"),
            P("dp", "mp"),
            P("mp", "dp"),
            P("mp", "dp"),
            P(None, "dp"),
            P(None, "dp"),
        ),
        out_specs=(
            P("dp", None),
            P("dp", None),
            P(),
            P(None, "dp", "mp"),
            P(None, "dp", "mp"),
            P(None, "dp", "mp"),
            P("mp", "dp"),
            P("mp", "dp"),
            P("mp", "dp"),
            P("dp", "mp"),
            P("dp", "mp"),
            P("dp", "mp"),
            P("mp", "dp"),
            P("mp", "dp"),
            P("mp", "dp"),
            P(None, "dp"),
            P(None, "dp"),
            P(None, "dp"),
            P(None, "dp"),
        ),
        check_vma=False,
    )
```
